512 devices in a mesh: ep: 128 (over z, y, core), dp: 4 (over x).
Axes of the slice: x: 4, y: 8, z: 8, core: 2. Of those that a mesh axis runs over, the one named last changes fastest.
Arguments:
- tokens: bfloat16 [4, 512, 3584], P(None, ('ep', 'dp')), may hold values from -6 to 6
- route_weight: bfloat16 [4, 512, 8], P(None, ('ep', 'dp')), may hold values from 0.049804688 to 0.5
- expert_ids: int32 [4, 512, 8], P(None, ('ep', 'dp')), may hold values from 0 to 55, all different within a row; in each aligned block of 4 rows (0 to 3, 4 to 7, ..., all dimensions but the last counted through in order) at most 2 rows name the same one
- replica: int32 [4, 512, 8], P(None, ('ep', 'dp')), may hold values from 0 to 1
- placement: int32 [56, 2], replicated, may hold values from 0 to 63, as said below
- w_gate: bfloat16 [128, 3584, 512], P('ep', None, 'dp'), as said below
- w_up: bfloat16 [128, 3584, 512], P('ep', None, 'dp'), as said below
- w_down: bfloat16 [128, 512, 3584], P('ep', 'dp'), as said below
Outputs:
- moe_out: bfloat16 [4, 512, 3584], P(None, ('ep', 'dp'))
- slot_rows: int32 [4, 128], P(None, 'ep')
The draws below stay inside these ranges and needn't reach their ends.
Inputs may be any that keep to these rules, and one draw needn't show every extreme that they name: `expert_ids`: in each aligned block of 4 rows (the tokens of one ep index at one step), no expert is named by more than 2 tokens; in some blocks one expert is named by exactly 2. `placement`: every slot holds exactly one expert; 8 experts have two different slots, the others have the same slot in both columns. `w_gate`: two slots of one expert hold equal weights. `w_up`: two slots of one expert hold equal weights. `w_down`: two slots of one expert hold equal weights.
All inputs are finite; a program needn't handle non-finite values.
Results may differ from the reference program's by a relative error of at most 0.0059.
Values may be sent and summed in bfloat16 or wider, within the bound.
No kernel may reach another device: no remote copies, remote signals or barrier semaphores. Data moves between devices by JAX's collectives and lax.ppermute only.
A program may use at most 128 MiB of HBM per device.

```python
import math
import jax
import jax.numpy as jnp
import numpy as np
from jax import lax

D = 3584
FF = 1024
STEPS = 4
SLOTS = 64
REDUNDANT = 8
LOGICAL = 56
TOP = 8
GROUP = 4
CAP = 2
HID = 128
TOKENS = 512
N_EP = 128
N_DP = 4


def plan_slots(key):
    shuffled = jax.random.permutation(key, SLOTS).astype(jnp.int32)
    copied = jax.random.permutation(jax.random.fold_in(key, 1), LOGICAL)[:REDUNDANT].astype(jnp.int32)
    primary = shuffled[:LOGICAL]
    second = primary.at[copied].set(shuffled[LOGICAL:])
    owners = jnp.zeros((SLOTS,), jnp.int32).at[primary].set(jnp.arange(LOGICAL, dtype=jnp.int32))
    owners = owners.at[shuffled[LOGICAL:]].set(copied)
    return (primary, second, owners)


def expert_matrix(key, owners, row_count, column_count, factor):

    def one_device(device):
        expert_key = jax.random.fold_in(jax.random.fold_in(key, owners[device // 2]), device % 2)
        return jax.random.normal(expert_key, (row_count, column_count), jnp.float32) * factor
    return jax.vmap(one_device)(jnp.arange(N_EP, dtype=jnp.int32))


def draw_placement(key, part):
    primary, second, owners = plan_slots(key)
    return jnp.stack([primary, second], axis=1).astype(jnp.int32)


def draw_w_gate(key, part):
    owners = plan_slots(key)[2]
    key = jax.random.fold_in(key, 11)
    return expert_matrix(key, owners, D, FF // 2, D ** (-0.5)).astype(jnp.bfloat16)


def draw_w_up(key, part):
    owners = plan_slots(key)[2]
    key = jax.random.fold_in(key, 12)
    return expert_matrix(key, owners, D, FF // 2, D ** (-0.5)).astype(jnp.bfloat16)


def draw_w_down(key, part):
    owners = plan_slots(key)[2]
    key = jax.random.fold_in(key, 13)
    return expert_matrix(key, owners, FF // 2, D, FF ** (-0.5)).astype(jnp.bfloat16)


def plant(values, own_key, least, top_value):
    index_at = [jax.random.randint(jax.random.fold_in(own_key, axis), (), 0, length) for axis, length in enumerate(values.shape)]
    longest = values.shape.index(max(values.shape))
    next_to = index_at[:longest] + [(index_at[longest] + 1) % values.shape[longest]] + index_at[longest + 1:]
    return values.at[tuple(index_at)].set(least).at[tuple(next_to)].set(top_value)


def block_scale(key, shape, shards, least, top_value):
    def one(dim, shards_of):
        heights = jax.random.uniform(jax.random.fold_in(jax.random.fold_in(key, 6), dim), (shards_of,), jnp.float32, least / len(shards), top_value / len(shards))
        return jnp.repeat(jnp.exp(heights), shape[dim] // shards_of).reshape((-1,) + (1,) * (len(shape) - dim - 1))

    factor_of = one(*shards[0])
    for cut in shards[1:]:
        factor_of = factor_of * one(*cut)
    return factor_of


def assign_block(own_key, own, number, rows, amount, top, limit, lean):
    ranking = jax.random.permutation(own_key, amount)
    packed, common = portions_of(amount, rows * top, limit, lean, True), portions_of(amount, rows * top, limit, lean, False)
    places = jnp.arange(amount)

    def named(lengths, turn):
        used = int((lengths > 0).sum())
        fixed = max(1, used // 4)
        passed = fixed + (places - fixed + turn * (used - fixed)) % max(1, amount - fixed)
        return jnp.zeros((amount,), jnp.int32).at[ranking[jnp.where(places < fixed, places, passed)]].set(jnp.asarray(lengths, jnp.int32))

    lengths = jnp.where(number % 4 == 0, named(packed, number // 4), named(common, number - number // 4 - 1))
    mixed = jax.random.permutation(jax.random.fold_in(own, 3), amount)
    source_of, taker = mixed[0:amount // 2 * 2:2], mixed[1:amount // 2 * 2:2]
    room = jnp.minimum(lengths[source_of] - 1, limit - lengths[taker]) // 2
    room = jnp.where((source_of == ranking[0]) | (taker == ranking[0]) | (lengths[taker] == 0), 0, jnp.maximum(room, 0))
    passed = jax.random.randint(jax.random.fold_in(own, 4), (amount // 2,), 0, 1 << 20) % (room + 1)
    lengths = lengths.at[source_of].add(-passed).at[taker].add(passed)
    labels = jnp.searchsorted(jnp.cumsum(lengths), jnp.arange(rows * top), side="right").astype(jnp.int32)
    grid = labels.reshape(top, rows).T
    grid = grid[jax.random.permutation(jax.random.fold_in(own, 1), rows)]
    turn = jax.random.randint(jax.random.fold_in(own, 2), (rows, 1), 0, top)
    return jnp.take_along_axis(grid, (jnp.arange(top)[None, :] + turn) % top, axis=1)


def portions_of(amount, total, reach, slope, full):
    weights = [(1 << 20) // math.isqrt(rank ** slope) + 1 for rank in range(1, amount + 1)]
    largest = reach if full else min(reach, max(-(-total // amount), total * weights[0] // sum(weights)))
    least = 1 if total - largest >= amount - 1 else 0
    holding, spare = [largest] + [least] * (amount - 1), total - largest - least * (amount - 1)
    while spare > 0:
        candidates = [i for i in range(1, amount) if holding[i] < largest] or [i for i in range(1, amount) if holding[i] < reach]
        whole, left = sum([weights[i] for i in candidates]), spare
        for i in candidates:
            more = min(reach - holding[i], max(1, left * weights[i] // whole), spare)
            holding[i] = holding[i] + more
            spare = spare - more
    return np.array(holding)


def centred(rng, shape, width, limit, cuts=(), held_as=jnp.bfloat16):
    gain = block_scale(rng, shape, cuts, -0.22, 0.18) if cuts else 1.0
    entries = jax.random.normal(rng, shape, jnp.float32) * width * gain
    return jnp.minimum(jnp.maximum(entries, -limit), limit).astype(held_as)


def setup_inputs(seed: int = 0) -> dict:
    splits = jax.random.split(jax.random.key(seed), 9)
    tokens = centred(splits[0], (STEPS, TOKENS, D), 1.0, 6.0, ((1, 512),))
    route_weight = jnp.clip(jnp.exp(math.log(0.5) - 2.306499 * jax.random.uniform(splits[1], (STEPS, TOKENS, TOP), jnp.float32) ** block_scale(splits[1], (STEPS, TOKENS, TOP), ((1, 512),), -0.2, 0.2)), 0.049804688, 0.5).astype(jnp.bfloat16)
    expert_ids_keys = jax.random.split(jax.random.fold_in(splits[2], 1), STEPS * TOKENS // GROUP)
    expert_ids_turns = jax.random.permutation(jax.random.fold_in(splits[2], 3), STEPS * TOKENS // GROUP)
    expert_ids = jax.vmap(lambda own, number: assign_block(jax.random.fold_in(splits[2], 2), own, number, GROUP, LOGICAL, TOP, CAP, 2))(expert_ids_keys, expert_ids_turns).reshape((STEPS, TOKENS, TOP))
    replica = plant(jax.random.randint(splits[3], (STEPS, TOKENS, TOP), 0, 2), jax.random.fold_in(splits[3], 1), 0, 1).astype(jnp.int32)
    placement = draw_placement(jax.random.fold_in(splits[8], 71), 0)
    w_gate = draw_w_gate(jax.random.fold_in(splits[8], 71), 0)
    w_up = draw_w_up(jax.random.fold_in(splits[8], 71), 0)
    w_down = draw_w_down(jax.random.fold_in(splits[8], 71), 0)
    return {"tokens": tokens, "route_weight": route_weight, "expert_ids": expert_ids, "replica": replica, "placement": placement, "w_gate": w_gate, "w_up": w_up, "w_down": w_down}


def pick_slots(expert_ids, replica, placement):
    logical = placement.shape[0]
    chosen = jnp.where(replica[..., None] == 0, placement[:, 0], placement[:, 1])
    matches = expert_ids[..., None] == jnp.arange(logical, dtype=jnp.int32)
    return jnp.sum(jnp.where(matches, chosen, 0), axis=-1).astype(jnp.int32)


def place_rows(group_slots, slot_count):
    flat_slots = group_slots.reshape(-1)
    matches = (flat_slots[:, None] == jnp.arange(slot_count, dtype=jnp.int32)[None, :]).astype(jnp.int32)
    earlier = (jnp.cumsum(matches, axis=0) - matches).astype(jnp.int32)
    position = jnp.sum(earlier * matches, axis=1).astype(jnp.int32)
    counts = jnp.sum(matches, axis=0).astype(jnp.int32)
    return position.reshape(group_slots.shape), counts


def expert_pair(expert_rows, gate_pair, up_pair, down_pair):
    running = jnp.zeros((expert_rows.shape[0], down_pair.shape[2]), jnp.float32)
    for half_index in range(2):
        gate_out = jnp.dot(expert_rows, gate_pair[half_index], preferred_element_type=jnp.float32)
        up_out = jnp.dot(expert_rows, up_pair[half_index], preferred_element_type=jnp.float32)
        hidden = (jax.nn.silu(gate_out) * up_out).astype(jnp.bfloat16)
        for block_index in range(N_DP):
            block_start = block_index * HID
            block_out = jnp.dot(hidden[:, block_start:block_start + HID], down_pair[half_index, block_start:block_start + HID], preferred_element_type=jnp.float32).astype(jnp.bfloat16)
            running = running + block_out.astype(jnp.float32)
    return running


def reference(tokens, route_weight, expert_ids, replica, placement, w_gate, w_up, w_down):
    slot_table = pick_slots(expert_ids, replica, placement)
    group_index = jnp.arange(N_EP, dtype=jnp.int32)[:, None, None]
    outputs = []
    load_rows = []
    for step_index in range(STEPS):
        grouped = tokens[step_index].reshape(N_EP, GROUP, D)
        group_slots = slot_table[step_index].reshape(N_EP, GROUP, TOP)
        position, counts = jax.vmap(lambda one_group: place_rows(one_group, SLOTS))(group_slots)
        source = jnp.broadcast_to(grouped[:, :, None, :], (N_EP, GROUP, TOP, D))
        buffer = jnp.zeros((SLOTS, N_EP, CAP, D), tokens.dtype).at[group_slots, group_index, position].set(source)

        def per_slot(slot_index):
            gate_pair = lax.dynamic_slice_in_dim(w_gate, 2 * slot_index, 2, 0)
            up_pair = lax.dynamic_slice_in_dim(w_up, 2 * slot_index, 2, 0)
            down_pair = lax.dynamic_slice_in_dim(w_down, 2 * slot_index, 2, 0)
            expert_rows = lax.dynamic_index_in_dim(buffer, slot_index, 0, keepdims=False).reshape(N_EP * CAP, D)
            return expert_pair(expert_rows, gate_pair, up_pair, down_pair).reshape(N_EP, CAP, D)

        expert_out = lax.map(per_slot, jnp.arange(SLOTS, dtype=jnp.int32))
        picked = expert_out[group_slots, group_index, position]
        weights = route_weight[step_index].reshape(N_EP, GROUP, TOP).astype(jnp.float32)
        combined = jnp.sum(picked * weights[..., None], axis=2)
        outputs.append(combined.reshape(TOKENS, D).astype(jnp.bfloat16))
        load_rows.append(jnp.repeat(jnp.sum(counts, axis=0), 2).astype(jnp.int32))
    return jnp.stack(outputs), jnp.stack(load_rows)
```

```python
import functools

import jax
import jax.numpy as jnp
from jax import lax
from jax.experimental import pallas as pl
from jax.experimental.pallas import tpu as pltpu
from jax.sharding import PartitionSpec as P

BF16 = jnp.bfloat16
F32 = jnp.float32
EMPTY = 256.0


VMEM = pl.BlockSpec(memory_space=pltpu.VMEM)
HBM = pl.BlockSpec(memory_space=pltpu.HBM)
SMEM = pl.BlockSpec(memory_space=pltpu.SMEM)


def call(body, outs, args, flops=0, in_specs=None, out_specs=None, scratch=()):
    moved = sum(a.size * a.dtype.itemsize for a in args)
    moved += sum(o.size * o.dtype.itemsize for o in outs)
    return pl.pallas_call(
        body,
        out_shape=tuple(outs),
        in_specs=in_specs or [VMEM] * len(args),
        out_specs=tuple(out_specs or [VMEM] * len(outs)),
        scratch_shapes=list(scratch),
        compiler_params=pltpu.CompilerParams(vmem_limit_bytes=40 * 1024 * 1024),
        cost_estimate=pl.CostEstimate(flops=flops, bytes_accessed=moved, transcendentals=0),
    )(*args)


def route_body(
    tok_hbm, weight_hbm, ids_hbm, replica_hbm, place_hbm, send_hbm,
    tok_ref, weight_ref, ids_ref, replica_ref, place_ref, send_ref, sems,
):
    pairs = [
        (place_hbm, place_ref),
        (ids_hbm, ids_ref),
        (replica_hbm, replica_ref),
        (weight_hbm, weight_ref),
        (tok_hbm, tok_ref),
    ]
    copies = [pltpu.make_async_copy(a, b, sems.at[i]) for i, (a, b) in enumerate(pairs)]
    for c in copies:
        c.start()
    for c in copies:
        c.wait()
    dp, steps, wide = send_ref.shape
    piece = wide - 128
    top = ids_ref.shape[2]
    logical = place_ref.shape[1]
    ids, replica = ids_ref[:, 0, :], replica_ref[:, 0, :]
    first = jnp.broadcast_to(place_ref[0:1, :], (steps, logical))
    second = jnp.broadcast_to(place_ref[1:2, :], (steps, logical))
    expert = lax.broadcasted_iota(jnp.int32, (steps, logical), 1)
    lane = lax.broadcasted_iota(jnp.int32, (steps, 128), 1)
    tail = jnp.zeros((steps, 128), F32)
    for k in range(top):
        chosen = jnp.where(replica[:, k : k + 1] == 0, first, second)
        picked = jnp.where(expert == ids[:, k : k + 1], chosen, 0)
        slot = jnp.sum(picked.astype(F32), axis=1, keepdims=True)
        tail = jnp.where(lane == k, slot, tail)
        tail = jnp.where(lane == top + k, weight_ref[:, k : k + 1].astype(F32), tail)
    tail = tail.astype(BF16)
    for x in range(dp):
        send_ref[x, :, :piece] = tok_ref[:, x * piece : (x + 1) * piece]
        send_ref[x, :, piece:] = tail
    out = pltpu.make_async_copy(send_ref, send_hbm, sems.at[len(pairs)])
    out.start()
    out.wait()


def pack_body(steps, capacity, top, got_ref, rows_hbm, weight_ref, rows_ref, sems):
    tokens = got_ref.shape[0]
    piece = got_ref.shape[1] - 128
    count = rows_ref.shape[0]
    per_slot = steps * capacity
    info = got_ref[:, piece:].astype(F32).T
    row = lax.broadcasted_iota(jnp.int32, (count, tokens), 0)
    col = lax.broadcasted_iota(jnp.int32, (count, tokens), 1)
    slot = (row // per_slot).astype(F32)
    same_step = (row % per_slot) // capacity == col % steps
    place = row % capacity
    weight = jnp.zeros((count, tokens), F32)
    match = jnp.zeros((count, tokens), F32)
    for k in range(top):
        here = slot == info[k : k + 1, :]
        match += here.astype(F32)
        weight += jnp.where(here, info[top + k : top + k + 1, :], 0.0)
    match = jnp.where(same_step, match, 0.0)
    a = lax.broadcasted_iota(jnp.int32, (tokens, tokens), 0)
    b = lax.broadcasted_iota(jnp.int32, (tokens, tokens), 1)
    earlier = ((a % steps == b % steps) & (a < b)).astype(F32).astype(BF16)
    before = jnp.dot(match.astype(BF16), earlier, preferred_element_type=F32)
    taken = (match > 0.5) & (before.astype(jnp.int32) == place)
    weight_ref[...] = jnp.where(taken, weight, 0.0).astype(BF16)
    pick = taken.astype(F32)
    used = jnp.sum(pick, axis=1, keepdims=True)
    pick = pick.astype(BF16)
    head = jnp.dot(pick, got_ref[:, :128], preferred_element_type=F32)
    lane = lax.broadcasted_iota(jnp.int32, (count, 128), 1)
    head = jnp.where((lane == 0) & (used < 0.5), EMPTY, head)
    rows_ref[:, :128] = head.astype(BF16)
    rows_ref[:, 128:] = jnp.dot(pick, got_ref[:, 128:piece], preferred_element_type=F32).astype(BF16)
    out = pltpu.make_async_copy(rows_ref, rows_hbm, sems.at[0])
    out.start()
    out.wait()


def gate_up_body(steps, capacity, here_ref, x_ref, *refs):
    dp = (len(refs) - 4) // 2
    w_refs = refs[: 2 * dp]
    out_hbm, count_ref, part_ref, sems = refs[2 * dp :]
    total = x_ref.shape[0]
    rows = total // dp
    cols = w_refs[0].shape[1]
    head = x_ref[:, :128]
    used = (head[:, 0:1].astype(F32) < EMPTY).astype(F32)
    row = lax.broadcasted_iota(jnp.int32, (total, 128), 0)
    lane = lax.broadcasted_iota(jnp.int32, (total, 128), 1)
    counted = jnp.where((row // capacity) % steps == lane, used, 0.0)
    count = jnp.sum(counted, axis=0, keepdims=True)
    count_ref[...] = jnp.broadcast_to(count, count_ref.shape)
    head = jnp.where(lane == 0, head.astype(F32) * used, head.astype(F32)).astype(BF16)
    x = jnp.concatenate([head, x_ref[:, 128:]], axis=1)
    copies = []
    for b, w_ref in enumerate(w_refs):
        h, d = b // dp, b % dp
        block = lax.rem(here_ref[0] - d + dp, dp) + h * dp
        part = jnp.dot(x, w_ref[...], preferred_element_type=F32).astype(BF16)
        for i in range(dp):
            part_ref[b, i] = part[i * rows : (i + 1) * rows]
        at = pl.multiple_of(block * cols, cols)
        out = pltpu.make_async_copy(part_ref.at[b], out_hbm.at[:, :, pl.ds(at, cols)], sems.at[b])
        out.start()
        copies.append(out)
    for out in copies:
        out.wait()


def hidden_body(got_ref, out_ref):
    parts, rows, cols = got_ref.shape
    for b in range(cols // 256):
        gate = jnp.zeros((rows, 128), F32)
        up = jnp.zeros((rows, 128), F32)
        for i in range(parts):
            gate += got_ref[i, :, b * 256 : b * 256 + 128].astype(F32)
            up += got_ref[i, :, b * 256 + 128 : b * 256 + 256].astype(F32)
        hidden = (gate / (1.0 + jnp.exp(-gate)) * up).astype(BF16)
        for i in range(parts):
            out_ref[i, :, b * 128 : b * 128 + 128] = hidden


def down_body(here_ref, hid_ref, *refs):
    dp = (len(refs) - 4) // 2
    w_refs = refs[: 2 * dp]
    out_hbm, w_all, out_ref = refs[2 * dp : 2 * dp + 3]
    sems = refs[2 * dp + 3]
    hid = w_refs[0].shape[0]
    for b, w_ref in enumerate(w_refs):
        h, d = b // dp, b % dp
        block = lax.rem(here_ref[0] - d + dp, dp) + h * dp
        w_all[pl.ds(pl.multiple_of(block * hid, hid), hid), :] = w_ref[...]
    total = out_ref.shape[0]
    pieces = 2
    rows = total // pieces
    copies = []
    for i in range(pieces):
        at = slice(i * rows, (i + 1) * rows)
        out_ref[at] = jnp.dot(hid_ref[at], w_all[...], preferred_element_type=F32).astype(BF16)
        out = pltpu.make_async_copy(out_ref.at[at], out_hbm.at[at], sems.at[i])
        out.start()
        copies.append(out)
    for out in copies:
        out.wait()


def combine_body(weight_ref, got_ref, out_ref):
    out = lax.dot_general(
        weight_ref[...], got_ref[...], (((0,), (0,)), ((), ())), preferred_element_type=F32
    )
    out_ref[...] = out.astype(BF16)


def blocks_over_dp(pick, here, dp):
    out = [pick(here)]
    for d in range(1, dp):
        block = pick(lax.rem(here + d, dp))
        out.append(lax.ppermute(block, "dp", [(x, (x + d) % dp) for x in range(dp)]))
    return out


def local(tokens, route_weight, expert_ids, replica, placement, w_gate, w_up, w_down):
    steps, _, width = tokens.shape
    top = expert_ids.shape[2]
    ep = lax.axis_size("ep")
    dp = lax.axis_size("dp")
    here = lax.axis_index("dp").astype(jnp.int32)
    slots = ep // 2
    piece = width // dp
    hid = w_gate.shape[2]
    capacity = 2
    per_slot = steps * capacity
    count = slots * per_slot
    same_core = [list(range(c, ep, 2)) for c in range(2)]
    swap = [(e, e ^ 1) for e in range(ep)]
    shape = jax.ShapeDtypeStruct
    here_at = here.reshape(1)

    (send,) = call(
        route_body,
        [shape((dp, steps, piece + 128), BF16)],
        [
            tokens.reshape(steps, width),
            route_weight.reshape(steps, top),
            expert_ids,
            replica,
            placement.T,
        ],
        in_specs=[HBM] * 5,
        out_specs=[HBM],
        scratch=[
            pltpu.VMEM((steps, width), BF16),
            pltpu.VMEM((steps, top), BF16),
            pltpu.VMEM((steps, 1, top), jnp.int32),
            pltpu.VMEM((steps, 1, top), jnp.int32),
            pltpu.VMEM(placement.shape[::-1], jnp.int32),
            pltpu.VMEM((dp, steps, piece + 128), BF16),
            pltpu.SemaphoreType.DMA((6,)),
        ],
    )
    got = lax.all_to_all(send, "dp", 0, 0)

    gate, up, down = w_gate[0], w_up[0], w_down[0]

    def gate_up_of(x):
        at = (x * piece, 0)
        size = (piece, hid)
        return jnp.concatenate([lax.dynamic_slice(gate, at, size), lax.dynamic_slice(up, at, size)], axis=1)

    gate_up = blocks_over_dp(gate_up_of, here, dp)
    gate_up_all = gate_up + [lax.ppermute(w, "ep", swap) for w in gate_up]
    down_of = lambda x: lax.dynamic_slice(down, (0, x * piece), (hid, piece))
    down_own = blocks_over_dp(down_of, here, dp)
    down_all = down_own + [lax.ppermute(w, "ep", swap) for w in down_own]

    rows, weight = call(
        functools.partial(pack_body, steps, capacity, top),
        [shape((count, piece), BF16), shape((count, dp * steps), BF16)],
        [got.reshape(dp * steps, piece + 128)],
        out_specs=[HBM, VMEM],
        scratch=[pltpu.VMEM((count, piece), BF16), pltpu.SemaphoreType.DMA((1,))],
    )
    arrived = lax.all_to_all(
        rows.reshape(slots, per_slot, piece), "ep", 0, 0, axis_index_groups=same_core
    ).reshape(count, piece)

    partial, used = call(
        functools.partial(gate_up_body, steps, capacity),
        [shape((dp, count // dp, 4 * dp * hid), BF16), shape((8, 128), F32)],
        [here_at, arrived, *gate_up_all],
        2 * count * piece * 4 * dp * hid,
        in_specs=[SMEM] + [VMEM] * (2 * dp + 1),
        out_specs=[HBM, VMEM],
        scratch=[
            pltpu.VMEM((2 * dp, dp, count // dp, 2 * hid), BF16),
            pltpu.SemaphoreType.DMA((2 * dp,)),
        ],
    )
    partial = lax.all_to_all(partial, "dp", 0, 0)
    (hidden,) = call(hidden_body, [shape((dp, count // dp, 2 * dp * hid), BF16)], [partial])
    hidden = lax.all_to_all(hidden, "dp", 0, 0).reshape(count, 2 * dp * hid)
    (out,) = call(
        down_body,
        [shape((count, piece), BF16)],
        [here_at, hidden, *down_all],
        4 * count * piece * dp * hid,
        in_specs=[SMEM] + [VMEM] * (2 * dp + 1),
        out_specs=[HBM],
        scratch=[
            pltpu.VMEM((2 * dp * hid, piece), BF16),
            pltpu.VMEM((count, piece), BF16),
            pltpu.SemaphoreType.DMA((2,)),
        ],
    )
    returned = lax.all_to_all(
        out.reshape(slots, per_slot, piece), "ep", 0, 0, axis_index_groups=same_core
    ).reshape(count, piece)
    (mine,) = call(combine_body, [shape((dp * steps, piece), BF16)], [weight, returned])
    mine = lax.all_to_all(mine.reshape(dp, steps, piece), "dp", 0, 0)
    moe_out = jnp.transpose(mine, (1, 0, 2)).reshape(steps, 1, width)

    used_there = lax.ppermute(used, "ep", swap)
    slot_rows = (used + used_there)[0, :steps].astype(jnp.int32).reshape(steps, 1)
    return (moe_out, slot_rows)


def solution(mesh):
    return jax.shard_map(
        local,
        mesh=mesh,
        in_specs=(
            P(None, ("ep", "dp"), None),
            P(None, ("ep", "dp"), None),
            P(None, ("ep", "dp"), None),
            P(None, ("ep", "dp"), None),
            P(),
            P("ep", None, "dp"),
            P("ep", None, "dp"),
            P("ep", "dp", None),
        ),
        out_specs=(P(None, ("ep", "dp"), None), P(None, "ep")),
        check_vma=False,
    )
```

```python
import functools

import jax
import jax.numpy as jnp
from jax import lax
from jax.experimental import pallas as pl
from jax.experimental.pallas import tpu as pltpu
from jax.sharding import PartitionSpec as P

BF16 = jnp.bfloat16
F32 = jnp.float32
EMPTY = 256.0


VMEM = pl.BlockSpec(memory_space=pltpu.VMEM)
HBM = pl.BlockSpec(memory_space=pltpu.HBM)
ANY = pl.BlockSpec(memory_space=pl.ANY)
SMEM = pl.BlockSpec(memory_space=pltpu.SMEM)


def call(body, outs, args, flops=0, in_specs=None, out_specs=None, scratch=()):
    if in_specs:
        args = [
            pltpu.with_memory_space_constraint(a, pltpu.HBM) if spec is HBM else a
            for a, spec in zip(args, in_specs, strict=True)
        ]
    moved = sum(a.size * a.dtype.itemsize for a in args)
    moved += sum(o.size * o.dtype.itemsize for o in outs)
    return pl.pallas_call(
        body,
        out_shape=tuple(
            pltpu.HBM(o.shape, o.dtype) if spec is HBM else o
            for o, spec in zip(outs, out_specs or [VMEM] * len(outs), strict=True)
        ),
        in_specs=in_specs or [VMEM] * len(args),
        out_specs=tuple(out_specs or [VMEM] * len(outs)),
        scratch_shapes=list(scratch),
        compiler_params=pltpu.CompilerParams(vmem_limit_bytes=40 * 1024 * 1024),
        cost_estimate=pl.CostEstimate(flops=flops, bytes_accessed=moved, transcendentals=0),
    )(*args)


def route_body(
    tok_hbm, weight_hbm, ids_hbm, replica_hbm, place_hbm, send_hbm,
    tok_ref, weight_ref, ids_ref, replica_ref, place_ref, send_ref, sems,
):
    pairs = [
        (place_hbm, place_ref),
        (ids_hbm, ids_ref),
        (replica_hbm, replica_ref),
        (weight_hbm, weight_ref),
        (tok_hbm, tok_ref),
    ]
    copies = [pltpu.make_async_copy(a, b, sems.at[i]) for i, (a, b) in enumerate(pairs)]
    for c in copies:
        c.start()
    for c in copies:
        c.wait()
    dp, steps, wide = send_ref.shape
    piece = wide - 128
    top = ids_ref.shape[2]
    logical = place_ref.shape[1]
    ids, replica = ids_ref[:, 0, :], replica_ref[:, 0, :]
    first = jnp.broadcast_to(place_ref[0:1, :], (steps, logical))
    second = jnp.broadcast_to(place_ref[1:2, :], (steps, logical))
    expert = lax.broadcasted_iota(jnp.int32, (steps, logical), 1)
    lane = lax.broadcasted_iota(jnp.int32, (steps, 128), 1)
    tail = jnp.zeros((steps, 128), F32)
    for k in range(top):
        chosen = jnp.where(replica[:, k : k + 1] == 0, first, second)
        picked = jnp.where(expert == ids[:, k : k + 1], chosen, 0)
        slot = jnp.sum(picked.astype(F32), axis=1, keepdims=True)
        tail = jnp.where(lane == k, slot, tail)
        tail = jnp.where(lane == top + k, weight_ref[:, k : k + 1].astype(F32), tail)
    tail = tail.astype(BF16)
    for x in range(dp):
        send_ref[x, :, :piece] = tok_ref[:, x * piece : (x + 1) * piece]
        send_ref[x, :, piece:] = tail
    out = pltpu.make_async_copy(send_ref, send_hbm, sems.at[len(pairs)])
    out.start()
    out.wait()


def pack_body(steps, capacity, top, got_ref, rows_hbm, weight_ref, rows_ref, sems):
    tokens = got_ref.shape[0]
    piece = got_ref.shape[1] - 128
    count = rows_ref.shape[0]
    per_slot = steps * capacity
    info = got_ref[:, piece:].astype(F32).T
    row = lax.broadcasted_iota(jnp.int32, (count, tokens), 0)
    col = lax.broadcasted_iota(jnp.int32, (count, tokens), 1)
    slot = (row // per_slot).astype(F32)
    same_step = (row % per_slot) // capacity == col % steps
    place = row % capacity
    weight = jnp.zeros((count, tokens), F32)
    match = jnp.zeros((count, tokens), F32)
    for k in range(top):
        here = slot == info[k : k + 1, :]
        match += here.astype(F32)
        weight += jnp.where(here, info[top + k : top + k + 1, :], 0.0)
    match = jnp.where(same_step, match, 0.0)
    a = lax.broadcasted_iota(jnp.int32, (tokens, tokens), 0)
    b = lax.broadcasted_iota(jnp.int32, (tokens, tokens), 1)
    earlier = ((a % steps == b % steps) & (a < b)).astype(F32).astype(BF16)
    before = jnp.dot(match.astype(BF16), earlier, preferred_element_type=F32)
    taken = (match > 0.5) & (before.astype(jnp.int32) == place)
    weight_ref[...] = jnp.where(taken, weight, 0.0).astype(BF16)
    pick = taken.astype(F32)
    used = jnp.sum(pick, axis=1, keepdims=True)
    pick = pick.astype(BF16)
    head = jnp.dot(pick, got_ref[:, :128], preferred_element_type=F32)
    lane = lax.broadcasted_iota(jnp.int32, (count, 128), 1)
    head = jnp.where((lane == 0) & (used < 0.5), EMPTY, head)
    rows_ref[:, :128] = head.astype(BF16)
    rows_ref[:, 128:] = jnp.dot(pick, got_ref[:, 128:piece], preferred_element_type=F32).astype(BF16)
    out = pltpu.make_async_copy(rows_ref, rows_hbm, sems.at[0])
    out.start()
    out.wait()


def select_body(
    steps, capacity, first, x_hbm, *refs
):
    kept_hbm, pick_ref, count_ref, total_ref, x_ref, kept_ref, sems = refs[-7:]
    load = pltpu.make_async_copy(x_hbm, x_ref, sems.at[0])
    load.start()
    load.wait()
    total = x_ref.shape[0]
    rows = kept_ref.shape[0]
    head = x_ref[:, :128]
    lane8 = lax.broadcasted_iota(jnp.int32, (8, 128), 1)
    leader = (lane8 == 0).astype(F32).astype(BF16)
    front = lax.dot_general(leader, head, (((1,), (1,)), ((), ())), preferred_element_type=F32)
    used = (front < EMPTY).astype(F32)
    a = lax.broadcasted_iota(jnp.int32, (total, total), 0)
    b = lax.broadcasted_iota(jnp.int32, (total, total), 1)
    before = (a < b).astype(F32).astype(BF16)
    rank = jnp.dot(used.astype(BF16), before, preferred_element_type=F32).astype(jnp.int32) - first
    want = lax.broadcasted_iota(jnp.int32, (rows, total), 0)
    pick = ((want == rank[0:1, :]) & (used[0:1, :] > 0.5)).astype(F32).astype(BF16)
    pick_ref[...] = pick
    kept_ref[...] = jnp.dot(pick, x_ref[...], preferred_element_type=F32).astype(BF16)
    copies = []
    for i in range(kept_hbm.shape[0]):
        copy = pltpu.make_async_copy(kept_ref, kept_hbm.at[i], sems.at[1 + i])
        copy.start()
        copies.append(copy)
    row = lax.broadcasted_iota(jnp.int32, (total, 128), 0)
    lane = lax.broadcasted_iota(jnp.int32, (total, 128), 1)
    its_step = ((row // capacity) % steps == lane).astype(F32).astype(BF16)
    count_ref[...] = jnp.dot(used.astype(BF16), its_step, preferred_element_type=F32)
    total_ref[...] = jnp.broadcast_to(jnp.sum(used, axis=1, keepdims=True), total_ref.shape).astype(jnp.int32)
    for copy in copies:
        copy.wait()


def hidden_body(x_ref, gate_ref, up_ref, gate_there_ref, up_there_ref, out_hbm, out_ref, sems):
    parts, rows, piece = x_ref.shape
    hid = gate_ref.shape[1]
    gate = jnp.zeros((rows, 2 * hid), F32)
    up = jnp.zeros((rows, 2 * hid), F32)
    for i in range(parts):
        at = slice(i * piece, (i + 1) * piece)
        x = x_ref[i]
        gate_w = jnp.concatenate([gate_ref[at, :], gate_there_ref[at, :]], axis=1)
        up_w = jnp.concatenate([up_ref[at, :], up_there_ref[at, :]], axis=1)
        gate += jnp.dot(x, gate_w, preferred_element_type=F32)
        up += jnp.dot(x, up_w, preferred_element_type=F32)
    out_ref[...] = (gate / (1.0 + jnp.exp(-gate)) * up).astype(BF16)
    copies = [pltpu.make_async_copy(out_ref, out_hbm.at[i], sems.at[i]) for i in range(parts)]
    for copy in copies:
        copy.start()
    for copy in copies:
        copy.wait()


def down_body(here_ref, hid_ref, pick_ref, own_ref, there_ref, out_hbm, out_ref, sems):
    dp, rows, _ = hid_ref.shape
    out = jnp.zeros((rows, own_ref.shape[2]), F32)
    for d in range(dp):
        block = lax.rem(here_ref[0] - d + dp, dp)
        w = jnp.concatenate([own_ref[d], there_ref[d]], axis=0)
        out += jnp.dot(hid_ref[block], w, preferred_element_type=F32)
    out = out.astype(BF16)
    total = out_ref.shape[0]
    pieces = 2
    size = total // pieces
    copies = []
    for i in range(pieces):
        at = slice(i * size, (i + 1) * size)
        spread = lax.dot_general(
            pick_ref[:, at], out, (((0,), (0,)), ((), ())), preferred_element_type=F32
        )
        out_ref[at] = spread.astype(BF16)
        copy = pltpu.make_async_copy(out_ref.at[at], out_hbm.at[at], sems.at[i])
        copy.start()
        copies.append(copy)
    for copy in copies:
        copy.wait()


def combine_body(weight_ref, got_ref, out_ref):
    dp, steps, _ = out_ref.shape
    out = lax.dot_general(
        weight_ref[...], got_ref[...], (((0,), (0,)), ((), ())), preferred_element_type=F32
    ).astype(BF16)
    for i in range(dp):
        out_ref[i] = out[i * steps : (i + 1) * steps]


def local(tokens, route_weight, expert_ids, replica, placement, w_gate, w_up, w_down):
    steps, _, width = tokens.shape
    top = expert_ids.shape[2]
    ep = lax.axis_size("ep")
    dp = lax.axis_size("dp")
    here = lax.axis_index("dp").astype(jnp.int32)
    slots = ep // 2
    piece = width // dp
    hid = w_gate.shape[2]
    capacity = 2
    per_slot = steps * capacity
    count = slots * per_slot
    kept = count // 2
    same_core = [list(range(c, ep, 2)) for c in range(2)]
    swap = [(e, e ^ 1) for e in range(ep)]
    shape = jax.ShapeDtypeStruct
    here_at = here.reshape(1)

    (send,) = call(
        route_body,
        [shape((dp, steps, piece + 128), BF16)],
        [
            tokens.reshape(steps, width),
            route_weight.reshape(steps, top),
            expert_ids,
            replica,
            placement.T,
        ],
        in_specs=[HBM] * 5,
        out_specs=[HBM],
        scratch=[
            pltpu.VMEM((steps, width), BF16),
            pltpu.VMEM((steps, top), BF16),
            pltpu.VMEM((steps, 1, top), jnp.int32),
            pltpu.VMEM((steps, 1, top), jnp.int32),
            pltpu.VMEM(placement.shape[::-1], jnp.int32),
            pltpu.VMEM((dp, steps, piece + 128), BF16),
            pltpu.SemaphoreType.DMA((6,)),
        ],
    )
    got = lax.all_to_all(send, "dp", 0, 0)

    gate, up, down = w_gate[0], w_up[0], w_down[0]
    gate_there = lax.ppermute(gate, "ep", swap)
    up_there = lax.ppermute(up, "ep", swap)
    down_own = []
    for d in range(dp):
        block = lax.dynamic_slice(down, (0, lax.rem(here + d, dp) * piece), (hid, piece))
        down_own.append(lax.ppermute(block, "dp", [(x, (x + d) % dp) for x in range(dp)]) if d else block)
    down_own = jnp.stack(down_own)
    down_there = lax.ppermute(down_own, "ep", swap)

    rows, weight = call(
        functools.partial(pack_body, steps, capacity, top),
        [shape((count, piece), BF16), shape((count, dp * steps), BF16)],
        [got.reshape(dp * steps, piece + 128)],
        out_specs=[HBM, VMEM],
        scratch=[pltpu.VMEM((count, piece), BF16), pltpu.SemaphoreType.DMA((1,))],
    )
    arrived = lax.all_to_all(
        rows.reshape(slots, per_slot, piece), "ep", 0, 0, axis_index_groups=same_core
    ).reshape(count, piece)

    def expert_rows(first, after):
        held, pick, used, total = call(
            functools.partial(select_body, steps, capacity, first),
            [
                shape((dp, kept, piece), BF16),
                shape((kept, count), BF16),
                shape((8, 128), F32),
                shape((8, 128), jnp.int32),
            ],
            [arrived, *after],
            2 * kept * count * piece,
            in_specs=[ANY] * (1 + len(after)),
            out_specs=[HBM, VMEM, VMEM, VMEM],
            scratch=[
                pltpu.VMEM((count, piece), BF16),
                pltpu.VMEM((kept, piece), BF16),
                pltpu.SemaphoreType.DMA((1 + dp,)),
            ],
        )
        held = lax.all_to_all(held, "dp", 0, 0)
        (hidden,) = call(
            hidden_body,
            [shape((dp, kept, 2 * hid), BF16)],
            [held, gate, up, gate_there, up_there],
            8 * kept * width * hid,
            out_specs=[HBM],
            scratch=[pltpu.VMEM((kept, 2 * hid), BF16), pltpu.SemaphoreType.DMA((dp,))],
        )
        hidden = lax.all_to_all(hidden, "dp", 0, 0)
        (out,) = call(
            down_body,
            [shape((count, piece), BF16)],
            [here_at, hidden, pick, down_own, down_there],
            4 * kept * piece * dp * hid,
            in_specs=[SMEM] + [VMEM] * 4,
            out_specs=[HBM],
            scratch=[pltpu.VMEM((count, piece), BF16), pltpu.SemaphoreType.DMA((2,))],
        )
        return out, used, total

    out, used, total = expert_rows(0, [down_there, gate_there, up_there])
    out = lax.cond(total[0, 0] > kept, lambda o: o + expert_rows(kept, [])[0], lambda o: o, out)
    returned = lax.all_to_all(
        out.reshape(slots, per_slot, piece), "ep", 0, 0, axis_index_groups=same_core
    ).reshape(count, piece)
    (mine,) = call(
        combine_body, [shape((dp, steps, piece), BF16)], [weight, returned]
    )
    mine = lax.all_to_all(mine, "dp", 0, 0)
    moe_out = jnp.transpose(mine, (1, 0, 2)).reshape(steps, 1, width)

    used_there = lax.ppermute(used, "ep", swap)
    slot_rows = (used + used_there)[0, :steps].astype(jnp.int32).reshape(steps, 1)
    return (moe_out, slot_rows)


def solution(mesh):
    return jax.shard_map(
        local,
        mesh=mesh,
        in_specs=(
            P(None, ("ep", "dp"), None),
            P(None, ("ep", "dp"), None),
            P(None, ("ep", "dp"), None),
            P(None, ("ep", "dp"), None),
            P(),
            P("ep", None, "dp"),
            P("ep", None, "dp"),
            P("ep", "dp", None),
        ),
        out_specs=(P(None, ("ep", "dp"), None), P(None, "ep")),
        check_vma=False,
    )
```

```python
import functools

import jax
import jax.numpy as jnp
from jax import lax
from jax.experimental import pallas as pl
from jax.experimental.pallas import tpu as pltpu
from jax.sharding import PartitionSpec as P

BF16 = jnp.bfloat16
F32 = jnp.float32
EMPTY = 256.0


VMEM = pl.BlockSpec(memory_space=pltpu.VMEM)
HBM = pl.BlockSpec(memory_space=pltpu.HBM)
ANY = pl.BlockSpec(memory_space=pl.ANY)
SMEM = pl.BlockSpec(memory_space=pltpu.SMEM)


def call(body, outs, args, flops=0, in_specs=None, out_specs=None, scratch=(), vmem=12):
    if in_specs:
        args = [
            pltpu.with_memory_space_constraint(a, pltpu.HBM) if spec is HBM else a
            for a, spec in zip(args, in_specs, strict=True)
        ]
    moved = sum(a.size * a.dtype.itemsize for a in args)
    moved += sum(o.size * o.dtype.itemsize for o in outs)
    return pl.pallas_call(
        body,
        out_shape=tuple(
            pltpu.HBM(o.shape, o.dtype) if spec is HBM else o
            for o, spec in zip(outs, out_specs or [VMEM] * len(outs), strict=True)
        ),
        in_specs=in_specs or [VMEM] * len(args),
        out_specs=tuple(out_specs or [VMEM] * len(outs)),
        scratch_shapes=list(scratch),
        compiler_params=pltpu.CompilerParams(vmem_limit_bytes=vmem * 1024 * 1024),
        cost_estimate=pl.CostEstimate(flops=flops, bytes_accessed=moved, transcendentals=0),
    )(*args)


def route_body(
    tok_hbm, weight_hbm, ids_hbm, replica_hbm, place_hbm, send_hbm,
    tok_ref, weight_ref, ids_ref, replica_ref, place_ref, send_ref, sems,
):
    pairs = [
        (place_hbm, place_ref),
        (ids_hbm, ids_ref),
        (replica_hbm, replica_ref),
        (weight_hbm, weight_ref),
        (tok_hbm, tok_ref),
    ]
    copies = [pltpu.make_async_copy(a, b, sems.at[i]) for i, (a, b) in enumerate(pairs)]
    for c in copies:
        c.start()
    for c in copies:
        c.wait()
    dp, steps, wide = send_ref.shape
    piece = wide - 128
    top = ids_ref.shape[2]
    logical = place_ref.shape[1]
    ids, replica = ids_ref[:, 0, :], replica_ref[:, 0, :]
    first = jnp.broadcast_to(place_ref[0:1, :], (steps, logical))
    second = jnp.broadcast_to(place_ref[1:2, :], (steps, logical))
    expert = lax.broadcasted_iota(jnp.int32, (steps, logical), 1)
    lane = lax.broadcasted_iota(jnp.int32, (steps, 128), 1)
    tail = jnp.zeros((steps, 128), F32)
    for k in range(top):
        chosen = jnp.where(replica[:, k : k + 1] == 0, first, second)
        picked = jnp.where(expert == ids[:, k : k + 1], chosen, 0)
        slot = jnp.sum(picked.astype(F32), axis=1, keepdims=True)
        tail = jnp.where(lane == k, slot, tail)
        tail = jnp.where(lane == top + k, weight_ref[:, k : k + 1].astype(F32), tail)
    tail = tail.astype(BF16)
    for x in range(dp):
        send_ref[x, :, :piece] = tok_ref[:, x * piece : (x + 1) * piece]
        send_ref[x, :, piece:] = tail
    out = pltpu.make_async_copy(send_ref, send_hbm, sems.at[len(pairs)])
    out.start()
    out.wait()


def pack_body(steps, capacity, top, got_ref, rows_hbm, weight_ref, rows_ref, sems):
    tokens = got_ref.shape[0]
    piece = got_ref.shape[1] - 128
    count = rows_ref.shape[0]
    per_slot = steps * capacity
    info = got_ref[:, piece:].astype(F32).T
    row = lax.broadcasted_iota(jnp.int32, (count, tokens), 0)
    col = lax.broadcasted_iota(jnp.int32, (count, tokens), 1)
    slot = (row // per_slot).astype(F32)
    same_step = (row % per_slot) // capacity == col % steps
    place = row % capacity
    weight = jnp.zeros((count, tokens), F32)
    match = jnp.zeros((count, tokens), F32)
    for k in range(top):
        here = slot == info[k : k + 1, :]
        match += here.astype(F32)
        weight += jnp.where(here, info[top + k : top + k + 1, :], 0.0)
    match = jnp.where(same_step, match, 0.0)
    a = lax.broadcasted_iota(jnp.int32, (tokens, tokens), 0)
    b = lax.broadcasted_iota(jnp.int32, (tokens, tokens), 1)
    earlier = ((a % steps == b % steps) & (a < b)).astype(F32).astype(BF16)
    before = jnp.dot(match.astype(BF16), earlier, preferred_element_type=F32)
    taken = (match > 0.5) & (before.astype(jnp.int32) == place)
    weight_ref[...] = jnp.where(taken, weight, 0.0).astype(BF16)
    pick = taken.astype(F32)
    used = jnp.sum(pick, axis=1, keepdims=True)
    pick = pick.astype(BF16)
    head = jnp.dot(pick, got_ref[:, :128], preferred_element_type=F32)
    lane = lax.broadcasted_iota(jnp.int32, (count, 128), 1)
    head = jnp.where((lane == 0) & (used < 0.5), EMPTY, head)
    rows_ref[:, :128] = head.astype(BF16)
    rows_ref[:, 128:] = jnp.dot(pick, got_ref[:, 128:piece], preferred_element_type=F32).astype(BF16)
    out = pltpu.make_async_copy(rows_ref, rows_hbm, sems.at[0])
    out.start()
    out.wait()


def split_body(steps, capacity, x_ref, *refs):
    first_ref, second_ref, count_ref = refs[-3:]
    total = x_ref.shape[0]
    half = total // 2
    head = x_ref[:, :128].astype(F32)
    used = (head[:, 0:1] < EMPTY).astype(F32)
    row = lax.broadcasted_iota(jnp.int32, (total, 128), 0)
    lane = lax.broadcasted_iota(jnp.int32, (total, 128), 1)
    counted = jnp.where((row // capacity) % steps == lane, used, 0.0)
    count_ref[...] = jnp.broadcast_to(jnp.sum(counted, axis=0, keepdims=True), count_ref.shape)
    head = jnp.where(lane == 0, head * used, head).astype(BF16)
    for i, out_ref in enumerate((first_ref, second_ref)):
        at = slice(i * half, (i + 1) * half)
        out_ref[:, :128] = head[at]
        out_ref[:, 128:] = x_ref[at, 128:]


def add_products(here_ref, weights, parts, gate, up):
    gate_ref, up_ref, gate_there_ref, up_there_ref = weights
    dp = 4
    for distance, first_ref, second_ref in parts:
        piece = first_ref.shape[1]
        block = lax.rem(here_ref[0] + distance, dp)
        at = pl.ds(pl.multiple_of(block * piece, piece), piece)
        gate_w = jnp.concatenate([gate_ref[at, :], gate_there_ref[at, :]], axis=1)
        up_w = jnp.concatenate([up_ref[at, :], up_there_ref[at, :]], axis=1)
        x = jnp.concatenate([first_ref[...], second_ref[...]], axis=0)
        gate_part = jnp.dot(x, gate_w, preferred_element_type=F32)
        up_part = jnp.dot(x, up_w, preferred_element_type=F32)
        gate = gate_part if gate is None else gate + gate_part
        up = up_part if up is None else up + up_part
    return gate, up


def own_piece_body(here_ref, first_ref, second_ref, *refs):
    weights, (gate_out, up_out) = refs[:4], refs[4:]
    gate_out[...], up_out[...] = add_products(here_ref, weights, [(0, first_ref, second_ref)], None, None)


def near_pieces_body(
    here_ref, left_first, left_second, right_first, right_second, gate_in, up_in, *refs
):
    weights, (gate_out, up_out) = refs[:4], refs[4:]
    parts = [(3, left_first, left_second), (1, right_first, right_second)]
    gate_out[...], up_out[...] = add_products(here_ref, weights, parts, gate_in[...], up_in[...])


def last_piece_body(here_ref, first_ref, second_ref, gate_in, up_in, *refs):
    weights, (out_hbm, out_ref, sems) = refs[:4], refs[4:]
    parts = [(2, first_ref, second_ref)]
    gate, up = add_products(here_ref, weights, parts, gate_in[...], up_in[...])
    out_ref[...] = (gate / (1.0 + jnp.exp(-gate)) * up).astype(BF16)
    copies = [pltpu.make_async_copy(out_ref, out_hbm.at[i], sems.at[i]) for i in range(out_hbm.shape[0])]
    for copy in copies:
        copy.start()
    for copy in copies:
        copy.wait()


def down_body(here_ref, hid_ref, own_ref, there_ref, out_hbm, out_ref, sems):
    dp, total, _ = hid_ref.shape
    pieces = 2
    size = total // pieces
    copies = []
    for i in range(pieces):
        at = slice(i * size, (i + 1) * size)
        out = jnp.zeros((size, own_ref.shape[2]), F32)
        for d in range(dp):
            block = lax.rem(here_ref[0] - d + dp, dp)
            w = jnp.concatenate([own_ref[d], there_ref[d]], axis=0)
            out += jnp.dot(hid_ref[block, at], w, preferred_element_type=F32)
        out_ref[at] = out.astype(BF16)
        copy = pltpu.make_async_copy(out_ref.at[at], out_hbm.at[at], sems.at[i])
        copy.start()
        copies.append(copy)
    for copy in copies:
        copy.wait()


def combine_body(weight_ref, got_ref, out_ref):
    dp, steps, _ = out_ref.shape
    out = lax.dot_general(
        weight_ref[...], got_ref[...], (((0,), (0,)), ((), ())), preferred_element_type=F32
    ).astype(BF16)
    for i in range(dp):
        out_ref[i] = out[i * steps : (i + 1) * steps]


def local(tokens, route_weight, expert_ids, replica, placement, w_gate, w_up, w_down):
    steps, _, width = tokens.shape
    top = expert_ids.shape[2]
    ep = lax.axis_size("ep")
    dp = lax.axis_size("dp")
    here = lax.axis_index("dp").astype(jnp.int32)
    slots = ep // 2
    piece = width // dp
    hid = w_gate.shape[2]
    capacity = 2
    per_slot = steps * capacity
    count = slots * per_slot
    same_core = [list(range(c, ep, 2)) for c in range(2)]
    swap = [(e, e ^ 1) for e in range(ep)]
    shape = jax.ShapeDtypeStruct
    here_at = here.reshape(1)

    (send,) = call(
        route_body,
        [shape((dp, steps, piece + 128), BF16)],
        [
            tokens.reshape(steps, width),
            route_weight.reshape(steps, top),
            expert_ids,
            replica,
            placement.T,
        ],
        in_specs=[HBM] * 5,
        out_specs=[HBM],
        scratch=[
            pltpu.VMEM((steps, width), BF16),
            pltpu.VMEM((steps, top), BF16),
            pltpu.VMEM((steps, 1, top), jnp.int32),
            pltpu.VMEM((steps, 1, top), jnp.int32),
            pltpu.VMEM(placement.shape[::-1], jnp.int32),
            pltpu.VMEM((dp, steps, piece + 128), BF16),
            pltpu.SemaphoreType.DMA((6,)),
        ],
    )
    got = lax.all_to_all(send, "dp", 0, 0)

    gate, up, down = w_gate[0], w_up[0], w_down[0]
    gate_there = lax.ppermute(gate, "ep", swap)
    up_there = lax.ppermute(up, "ep", swap)
    down_own = []
    for d in range(dp):
        block = lax.dynamic_slice(down, (0, lax.rem(here + d, dp) * piece), (hid, piece))
        down_own.append(lax.ppermute(block, "dp", [(x, (x + d) % dp) for x in range(dp)]) if d else block)
    down_own = jnp.stack(down_own)
    down_there = lax.ppermute(down_own, "ep", swap)

    rows, weight = call(
        functools.partial(pack_body, steps, capacity, top),
        [shape((count, piece), BF16), shape((count, dp * steps), BF16)],
        [got.reshape(dp * steps, piece + 128)],
        out_specs=[HBM, VMEM],
        scratch=[pltpu.VMEM((count, piece), BF16), pltpu.SemaphoreType.DMA((1,))],
    )
    arrived = lax.all_to_all(
        rows.reshape(slots, per_slot, piece), "ep", 0, 0, axis_index_groups=same_core
    ).reshape(count, piece)

    after = [down_there, gate_there, up_there]
    half = shape((count // 2, piece), BF16)
    first, second, used = call(
        functools.partial(split_body, steps, capacity),
        [half, half, shape((8, 128), F32)],
        [arrived, *after],
        in_specs=[VMEM] + [ANY] * len(after),
    )
    ahead = [(x, (x + 1) % dp) for x in range(dp)]
    behind = [(x, (x - 1) % dp) for x in range(dp)]
    left_first = lax.ppermute(first, "dp", ahead)
    right_second = lax.ppermute(second, "dp", behind)
    left_second = lax.ppermute(second, "dp", ahead)
    right_first = lax.ppermute(first, "dp", behind)
    far_first = lax.ppermute(left_first, "dp", ahead)
    far_second = lax.ppermute(right_second, "dp", behind)
    weights = [gate, up, gate_there, up_there]
    sums = [shape((count, 2 * hid), F32)] * 2
    flops = 4 * count * piece * 2 * hid
    gate_sum, up_sum = call(
        own_piece_body, sums, [here_at, first, second, *weights], flops, in_specs=[SMEM] + [VMEM] * 6
    )
    gate_sum, up_sum = call(
        near_pieces_body,
        sums,
        [here_at, left_first, left_second, right_first, right_second, gate_sum, up_sum, *weights],
        2 * flops,
        in_specs=[SMEM] + [VMEM] * 10,
    )
    (hidden,) = call(
        last_piece_body,
        [shape((dp, count, 2 * hid), BF16)],
        [here_at, far_first, far_second, gate_sum, up_sum, *weights],
        flops,
        in_specs=[SMEM] + [VMEM] * 8,
        out_specs=[HBM],
        scratch=[pltpu.VMEM((count, 2 * hid), BF16), pltpu.SemaphoreType.DMA((dp,))],
    )
    hidden = lax.all_to_all(hidden, "dp", 0, 0)
    (out,) = call(
        down_body,
        [shape((count, piece), BF16)],
        [here_at, hidden, down_own, down_there],
        4 * count * piece * dp * hid,
        in_specs=[SMEM] + [VMEM] * 3,
        out_specs=[HBM],
        scratch=[pltpu.VMEM((count, piece), BF16), pltpu.SemaphoreType.DMA((2,))],
    )
    returned = lax.all_to_all(
        out.reshape(slots, per_slot, piece), "ep", 0, 0, axis_index_groups=same_core
    ).reshape(count, piece)
    (mine,) = call(
        combine_body, [shape((dp, steps, piece), BF16)], [weight, returned]
    )
    mine = lax.all_to_all(mine, "dp", 0, 0)
    moe_out = jnp.transpose(mine, (1, 0, 2)).reshape(steps, 1, width)

    used_there = lax.ppermute(used, "ep", swap)
    slot_rows = (used + used_there)[0, :steps].astype(jnp.int32).reshape(steps, 1)
    return (moe_out, slot_rows)


def solution(mesh):
    return jax.shard_map(
        local,
        mesh=mesh,
        in_specs=(
            P(None, ("ep", "dp"), None),
            P(None, ("ep", "dp"), None),
            P(None, ("ep", "dp"), None),
            P(None, ("ep", "dp"), None),
            P(),
            P("ep", None, "dp"),
            P("ep", None, "dp"),
            P("ep", "dp", None),
        ),
        out_specs=(P(None, ("ep", "dp"), None), P(None, "ep")),
        check_vma=False,
    )
```

```python
import functools

import jax
import jax.numpy as jnp
from jax import lax
from jax.experimental import pallas as pl
from jax.experimental.pallas import tpu as pltpu
from jax.sharding import PartitionSpec as P

BF16 = jnp.bfloat16
F32 = jnp.float32
EMPTY = 256.0


VMEM = pl.BlockSpec(memory_space=pltpu.VMEM)
HBM = pl.BlockSpec(memory_space=pltpu.HBM)
ANY = pl.BlockSpec(memory_space=pl.ANY)
SMEM = pl.BlockSpec(memory_space=pltpu.SMEM)


def call(body, outs, args, flops=0, in_specs=None, out_specs=None, scratch=(), vmem=12):
    if in_specs:
        args = [
            pltpu.with_memory_space_constraint(a, pltpu.HBM) if spec is HBM else a
            for a, spec in zip(args, in_specs, strict=True)
        ]
    moved = sum(a.size * a.dtype.itemsize for a in args)
    moved += sum(o.size * o.dtype.itemsize for o in outs)
    return pl.pallas_call(
        body,
        out_shape=tuple(
            pltpu.HBM(o.shape, o.dtype) if spec is HBM else o
            for o, spec in zip(outs, out_specs or [VMEM] * len(outs), strict=True)
        ),
        in_specs=in_specs or [VMEM] * len(args),
        out_specs=tuple(out_specs or [VMEM] * len(outs)),
        scratch_shapes=list(scratch),
        compiler_params=pltpu.CompilerParams(vmem_limit_bytes=vmem * 1024 * 1024),
        cost_estimate=pl.CostEstimate(flops=flops, bytes_accessed=moved, transcendentals=0),
    )(*args)


def route_body(
    tok_hbm, weight_hbm, ids_hbm, replica_hbm, place_hbm, send_hbm,
    tok_ref, weight_ref, ids_ref, replica_ref, place_ref, send_ref, sems,
):
    pairs = [
        (place_hbm, place_ref),
        (ids_hbm, ids_ref),
        (replica_hbm, replica_ref),
        (weight_hbm, weight_ref),
        (tok_hbm, tok_ref),
    ]
    copies = [pltpu.make_async_copy(a, b, sems.at[i]) for i, (a, b) in enumerate(pairs)]
    for c in copies:
        c.start()
    for c in copies:
        c.wait()
    dp, steps, wide = send_ref.shape
    piece = wide - 128
    top = ids_ref.shape[2]
    logical = place_ref.shape[1]
    ids, replica = ids_ref[:, 0, :], replica_ref[:, 0, :]
    first = jnp.broadcast_to(place_ref[0:1, :], (steps, logical))
    second = jnp.broadcast_to(place_ref[1:2, :], (steps, logical))
    expert = lax.broadcasted_iota(jnp.int32, (steps, logical), 1)
    lane = lax.broadcasted_iota(jnp.int32, (steps, 128), 1)
    tail = jnp.zeros((steps, 128), F32)
    for k in range(top):
        chosen = jnp.where(replica[:, k : k + 1] == 0, first, second)
        picked = jnp.where(expert == ids[:, k : k + 1], chosen, 0)
        slot = jnp.sum(picked.astype(F32), axis=1, keepdims=True)
        tail = jnp.where(lane == k, slot, tail)
        tail = jnp.where(lane == top + k, weight_ref[:, k : k + 1].astype(F32), tail)
    tail = tail.astype(BF16)
    for x in range(dp):
        send_ref[x, :, :piece] = tok_ref[:, x * piece : (x + 1) * piece]
        send_ref[x, :, piece:] = tail
    out = pltpu.make_async_copy(send_ref, send_hbm, sems.at[len(pairs)])
    out.start()
    out.wait()


def pack_body(steps, capacity, top, got_ref, rows_hbm, weight_ref, rows_ref, sems):
    tokens = got_ref.shape[0]
    piece = got_ref.shape[1] - 128
    count = rows_ref.shape[0]
    per_slot = steps * capacity
    info = got_ref[:, piece:].astype(F32).T
    row = lax.broadcasted_iota(jnp.int32, (count, tokens), 0)
    col = lax.broadcasted_iota(jnp.int32, (count, tokens), 1)
    slot = (row // per_slot).astype(F32)
    same_step = (row % per_slot) // capacity == col % steps
    place = row % capacity
    weight = jnp.zeros((count, tokens), F32)
    match = jnp.zeros((count, tokens), F32)
    for k in range(top):
        here = slot == info[k : k + 1, :]
        match += here.astype(F32)
        weight += jnp.where(here, info[top + k : top + k + 1, :], 0.0)
    match = jnp.where(same_step, match, 0.0)
    a = lax.broadcasted_iota(jnp.int32, (tokens, tokens), 0)
    b = lax.broadcasted_iota(jnp.int32, (tokens, tokens), 1)
    earlier = ((a % steps == b % steps) & (a < b)).astype(F32).astype(BF16)
    before = jnp.dot(match.astype(BF16), earlier, preferred_element_type=F32)
    taken = (match > 0.5) & (before.astype(jnp.int32) == place)
    weight_ref[...] = jnp.where(taken, weight, 0.0).astype(BF16)
    pick = taken.astype(F32)
    used = jnp.sum(pick, axis=1, keepdims=True)
    pick = pick.astype(BF16)
    head = jnp.dot(pick, got_ref[:, :128], preferred_element_type=F32)
    lane = lax.broadcasted_iota(jnp.int32, (count, 128), 1)
    head = jnp.where((lane == 0) & (used < 0.5), EMPTY, head)
    rows_ref[:, :128] = head.astype(BF16)
    rows_ref[:, 128:] = jnp.dot(pick, got_ref[:, 128:piece], preferred_element_type=F32).astype(BF16)
    out = pltpu.make_async_copy(rows_ref, rows_hbm, sems.at[0])
    out.start()
    out.wait()


def split_body(steps, capacity, x_ref, *refs):
    first_ref, second_ref, count_ref = refs[-3:]
    total = x_ref.shape[0]
    half = total // 2
    head = x_ref[:, :128].astype(F32)
    used = (head[:, 0:1] < EMPTY).astype(F32)
    row = lax.broadcasted_iota(jnp.int32, (total, 128), 0)
    lane = lax.broadcasted_iota(jnp.int32, (total, 128), 1)
    counted = jnp.where((row // capacity) % steps == lane, used, 0.0)
    count_ref[...] = jnp.broadcast_to(jnp.sum(counted, axis=0, keepdims=True), count_ref.shape)
    head = jnp.where(lane == 0, head * used, head).astype(BF16)
    for i, out_ref in enumerate((first_ref, second_ref)):
        at = slice(i * half, (i + 1) * half)
        out_ref[:, :128] = head[at]
        out_ref[:, 128:] = x_ref[at, 128:]


def load_piece(here_ref, distance, weights, w_ref, sems):
    piece = w_ref.shape[1]
    dp = weights[0].shape[0] // piece
    block = lax.rem(here_ref[0] + distance, dp)
    at = pl.ds(pl.multiple_of(block * piece, piece), piece)
    loads = [pltpu.make_async_copy(w.at[at], w_ref.at[i], sems.at[i]) for i, w in enumerate(weights)]
    for load in loads:
        load.start()
    return loads


def beside(loads, w_ref):
    for load in loads:
        load.wait()
    gate_w = jnp.concatenate([w_ref[0], w_ref[2]], axis=1)
    up_w = jnp.concatenate([w_ref[1], w_ref[3]], axis=1)
    return gate_w, up_w


def products(first_ref, second_ref, gate_w, up_w):
    x = jnp.concatenate([first_ref[...], second_ref[...]], axis=0)
    gate = jnp.dot(x, gate_w, preferred_element_type=F32)
    up = jnp.dot(x, up_w, preferred_element_type=F32)
    return gate, up


def own_piece_body(here_ref, first_ref, second_ref, *refs):
    weights, (gate_out, up_out, w_ref, sems) = refs[:4], refs[4:]
    loads = load_piece(here_ref, 0, weights, w_ref, sems)
    gate_out[...], up_out[...] = products(first_ref, second_ref, *beside(loads, w_ref))


def near_pieces_body(
    here_ref, left_first, left_second, right_first, right_second, gate_in, up_in, *refs
):
    weights, (own_hbm, there_hbm) = refs[:4], refs[4:6]
    gate_out, up_out, far_out, down_out, w_ref, sems, down_sems = refs[6:]
    dp, hid, _ = own_hbm.shape
    down_loads = []
    for d in range(dp):
        for i, source in enumerate((own_hbm, there_hbm)):
            to = down_out.at[d, pl.ds(i * hid, hid)]
            down_loads.append(pltpu.make_async_copy(source.at[d], to, down_sems.at[d, i]))
    loads = [load_piece(here_ref, d, weights, w_ref.at[i], sems.at[i]) for i, d in enumerate((3, 1, 2))]
    for load in down_loads:
        load.start()
    gate, up = products(left_first, left_second, *beside(loads[0], w_ref.at[0]))
    gate_out[...] = gate_in[...] + gate
    up_out[...] = up_in[...] + up
    gate, up = products(right_first, right_second, *beside(loads[1], w_ref.at[1]))
    gate_out[...] += gate
    up_out[...] += up
    far_out[0], far_out[1] = beside(loads[2], w_ref.at[2])
    for load in down_loads:
        load.wait()


def last_piece_body(first_ref, second_ref, gate_in, up_in, far_ref, out_hbm, out_ref, sems):
    gate, up = products(first_ref, second_ref, far_ref[0], far_ref[1])
    gate += gate_in[...]
    up += up_in[...]
    out_ref[...] = (gate / (1.0 + jnp.exp(-gate)) * up).astype(BF16)
    copies = [pltpu.make_async_copy(out_ref, out_hbm.at[i], sems.at[i]) for i in range(out_hbm.shape[0])]
    for copy in copies:
        copy.start()
    for copy in copies:
        copy.wait()


def down_body(here_ref, hid_ref, w_ref, out_hbm, out_ref, sems):
    dp, total, _ = hid_ref.shape
    pieces = 2
    size = total // pieces
    copies = []
    for i in range(pieces):
        at = slice(i * size, (i + 1) * size)
        out = jnp.zeros((size, out_ref.shape[1]), F32)
        for d in range(dp):
            block = lax.rem(here_ref[0] - d + dp, dp)
            out += jnp.dot(hid_ref[block, at], w_ref[d], preferred_element_type=F32)
        out_ref[at] = out.astype(BF16)
        copy = pltpu.make_async_copy(out_ref.at[at], out_hbm.at[at], sems.at[i])
        copy.start()
        copies.append(copy)
    for copy in copies:
        copy.wait()


def combine_body(weight_ref, got_ref, out_ref):
    dp, steps, _ = out_ref.shape
    out = lax.dot_general(
        weight_ref[...], got_ref[...], (((0,), (0,)), ((), ())), preferred_element_type=F32
    ).astype(BF16)
    for i in range(dp):
        out_ref[i] = out[i * steps : (i + 1) * steps]


def local(tokens, route_weight, expert_ids, replica, placement, w_gate, w_up, w_down):
    steps, _, width = tokens.shape
    top = expert_ids.shape[2]
    ep = lax.axis_size("ep")
    dp = lax.axis_size("dp")
    here = lax.axis_index("dp").astype(jnp.int32)
    slots = ep // 2
    piece = width // dp
    hid = w_gate.shape[2]
    capacity = 2
    per_slot = steps * capacity
    count = slots * per_slot
    same_core = [list(range(c, ep, 2)) for c in range(2)]
    swap = [(e, e ^ 1) for e in range(ep)]
    shape = jax.ShapeDtypeStruct
    here_at = here.reshape(1)

    (send,) = call(
        route_body,
        [shape((dp, steps, piece + 128), BF16)],
        [
            tokens.reshape(steps, width),
            route_weight.reshape(steps, top),
            expert_ids,
            replica,
            placement.T,
        ],
        in_specs=[HBM] * 5,
        out_specs=[HBM],
        scratch=[
            pltpu.VMEM((steps, width), BF16),
            pltpu.VMEM((steps, top), BF16),
            pltpu.VMEM((steps, 1, top), jnp.int32),
            pltpu.VMEM((steps, 1, top), jnp.int32),
            pltpu.VMEM(placement.shape[::-1], jnp.int32),
            pltpu.VMEM((dp, steps, piece + 128), BF16),
            pltpu.SemaphoreType.DMA((6,)),
        ],
    )
    got = lax.all_to_all(send, "dp", 0, 0)

    gate, up, down = w_gate[0], w_up[0], w_down[0]
    gate_there = lax.ppermute(gate, "ep", swap)
    up_there = lax.ppermute(up, "ep", swap)
    down_own = []
    for d in range(dp):
        block = lax.dynamic_slice(down, (0, lax.rem(here + d, dp) * piece), (hid, piece))
        down_own.append(lax.ppermute(block, "dp", [(x, (x + d) % dp) for x in range(dp)]) if d else block)
    down_own = jnp.stack(down_own)
    down_there = lax.ppermute(down_own, "ep", swap)

    rows, weight = call(
        functools.partial(pack_body, steps, capacity, top),
        [shape((count, piece), BF16), shape((count, dp * steps), BF16)],
        [got.reshape(dp * steps, piece + 128)],
        out_specs=[HBM, VMEM],
        scratch=[pltpu.VMEM((count, piece), BF16), pltpu.SemaphoreType.DMA((1,))],
    )
    arrived = lax.all_to_all(
        rows.reshape(slots, per_slot, piece), "ep", 0, 0, axis_index_groups=same_core
    ).reshape(count, piece)

    after = [down_there, gate_there, up_there]
    half = shape((count // 2, piece), BF16)
    first, second, used = call(
        functools.partial(split_body, steps, capacity),
        [half, half, shape((8, 128), F32)],
        [arrived, *after],
        in_specs=[VMEM, HBM, ANY, ANY],
    )
    ahead = [(x, (x + 1) % dp) for x in range(dp)]
    behind = [(x, (x - 1) % dp) for x in range(dp)]
    left_first = lax.ppermute(first, "dp", ahead)
    right_second = lax.ppermute(second, "dp", behind)
    left_second = lax.ppermute(second, "dp", ahead)
    right_first = lax.ppermute(first, "dp", behind)
    far_first = lax.ppermute(left_first, "dp", ahead)
    far_second = lax.ppermute(right_second, "dp", behind)
    weights = [gate, up, gate_there, up_there]
    sums = [shape((count, 2 * hid), F32)] * 2
    flops = 4 * count * piece * 2 * hid
    gate_sum, up_sum = call(
        own_piece_body,
        sums,
        [here_at, first, second, *weights],
        flops,
        in_specs=[SMEM, VMEM, VMEM] + [HBM] * 4,
        scratch=[pltpu.VMEM((4, piece, hid), BF16), pltpu.SemaphoreType.DMA((4,))],
    )
    gate_sum, up_sum, far_weights, down_weights = call(
        near_pieces_body,
        [*sums, shape((2, piece, 2 * hid), BF16), shape((dp, 2 * hid, piece), BF16)],
        [here_at, left_first, left_second, right_first, right_second, gate_sum, up_sum, *weights, down_own, down_there],
        2 * flops,
        in_specs=[SMEM] + [VMEM] * 6 + [HBM] * 6,
        scratch=[
            pltpu.VMEM((3, 4, piece, hid), BF16),
            pltpu.SemaphoreType.DMA((3, 4)),
            pltpu.SemaphoreType.DMA((dp, 2)),
        ],
        vmem=16,
    )
    (hidden,) = call(
        last_piece_body,
        [shape((dp, count, 2 * hid), BF16)],
        [far_first, far_second, gate_sum, up_sum, far_weights],
        flops,
        out_specs=[HBM],
        scratch=[pltpu.VMEM((count, 2 * hid), BF16), pltpu.SemaphoreType.DMA((dp,))],
    )
    hidden = lax.all_to_all(hidden, "dp", 0, 0)
    (out,) = call(
        down_body,
        [shape((count, piece), BF16)],
        [here_at, hidden, down_weights],
        4 * count * piece * dp * hid,
        in_specs=[SMEM, VMEM, VMEM],
        out_specs=[HBM],
        scratch=[pltpu.VMEM((count, piece), BF16), pltpu.SemaphoreType.DMA((2,))],
    )
    returned = lax.all_to_all(
        out.reshape(slots, per_slot, piece), "ep", 0, 0, axis_index_groups=same_core
    ).reshape(count, piece)
    (mine,) = call(
        combine_body, [shape((dp, steps, piece), BF16)], [weight, returned]
    )
    mine = lax.all_to_all(mine, "dp", 0, 0)
    moe_out = jnp.transpose(mine, (1, 0, 2)).reshape(steps, 1, width)

    used_there = lax.ppermute(used, "ep", swap)
    slot_rows = (used + used_there)[0, :steps].astype(jnp.int32).reshape(steps, 1)
    return (moe_out, slot_rows)


def solution(mesh):
    return jax.shard_map(
        local,
        mesh=mesh,
        in_specs=(
            P(None, ("ep", "dp"), None),
            P(None, ("ep", "dp"), None),
            P(None, ("ep", "dp"), None),
            P(None, ("ep", "dp"), None),
            P(),
            P("ep", None, "dp"),
            P("ep", None, "dp"),
            P("ep", "dp", None),
        ),
        out_specs=(P(None, ("ep", "dp"), None), P(None, "ep")),
        check_vma=False,
    )
```

```python
import functools

import jax
import jax.numpy as jnp
from jax import lax
from jax.experimental import pallas as pl
from jax.experimental.pallas import tpu as pltpu
from jax.sharding import PartitionSpec as P

BF16 = jnp.bfloat16
F32 = jnp.float32
EMPTY = 256.0


VMEM = pl.BlockSpec(memory_space=pltpu.VMEM)
HBM = pl.BlockSpec(memory_space=pltpu.HBM)
ANY = pl.BlockSpec(memory_space=pl.ANY)
SMEM = pl.BlockSpec(memory_space=pltpu.SMEM)


def call(body, outs, args, flops=0, in_specs=None, out_specs=None, scratch=(), vmem=12):
    if in_specs:
        args = [
            pltpu.with_memory_space_constraint(a, pltpu.HBM) if spec is HBM else a
            for a, spec in zip(args, in_specs, strict=True)
        ]
    moved = sum(a.size * a.dtype.itemsize for a in args)
    moved += sum(o.size * o.dtype.itemsize for o in outs)
    return pl.pallas_call(
        body,
        out_shape=tuple(
            pltpu.HBM(o.shape, o.dtype) if spec is HBM else o
            for o, spec in zip(outs, out_specs or [VMEM] * len(outs), strict=True)
        ),
        in_specs=in_specs or [VMEM] * len(args),
        out_specs=tuple(out_specs or [VMEM] * len(outs)),
        scratch_shapes=list(scratch),
        compiler_params=pltpu.CompilerParams(vmem_limit_bytes=vmem * 1024 * 1024),
        cost_estimate=pl.CostEstimate(flops=flops, bytes_accessed=moved, transcendentals=0),
    )(*args)


def route_body(
    tok_hbm, weight_hbm, ids_hbm, replica_hbm, place_hbm, send_ref,
    tok_ref, weight_ref, ids_ref, replica_ref, place_ref, sems,
):
    pairs = [
        (place_hbm, place_ref),
        (ids_hbm, ids_ref),
        (replica_hbm, replica_ref),
        (weight_hbm, weight_ref),
        (tok_hbm, tok_ref),
    ]
    copies = [pltpu.make_async_copy(a, b, sems.at[i]) for i, (a, b) in enumerate(pairs)]
    for c in copies:
        c.start()
    for c in copies:
        c.wait()
    dp, steps, wide = send_ref.shape
    piece = wide - 128
    top = ids_ref.shape[2]
    logical = place_ref.shape[1]
    ids, replica = ids_ref[:, 0, :], replica_ref[:, 0, :]
    first = jnp.broadcast_to(place_ref[0:1, :], (steps, logical))
    second = jnp.broadcast_to(place_ref[1:2, :], (steps, logical))
    expert = lax.broadcasted_iota(jnp.int32, (steps, logical), 1)
    lane = lax.broadcasted_iota(jnp.int32, (steps, 128), 1)
    tail = jnp.zeros((steps, 128), F32)
    for k in range(top):
        chosen = jnp.where(replica[:, k : k + 1] == 0, first, second)
        picked = jnp.where(expert == ids[:, k : k + 1], chosen, 0)
        slot = jnp.sum(picked.astype(F32), axis=1, keepdims=True)
        tail = jnp.where(lane == k, slot, tail)
        tail = jnp.where(lane == top + k, weight_ref[:, k : k + 1].astype(F32), tail)
    tail = tail.astype(BF16)
    for x in range(dp):
        send_ref[x, :, :piece] = tok_ref[:, x * piece : (x + 1) * piece]
        send_ref[x, :, piece:] = tail


def pack_body(steps, capacity, top, got_ref, rows_hbm, weight_ref, rows_ref, sems):
    tokens = got_ref.shape[0]
    piece = got_ref.shape[1] - 128
    count = rows_ref.shape[0]
    per_slot = steps * capacity
    info = got_ref[:, piece:].astype(F32).T
    row = lax.broadcasted_iota(jnp.int32, (count, tokens), 0)
    col = lax.broadcasted_iota(jnp.int32, (count, tokens), 1)
    slot = (row // per_slot).astype(F32)
    same_step = (row % per_slot) // capacity == col % steps
    place = row % capacity
    weight = jnp.zeros((count, tokens), F32)
    match = jnp.zeros((count, tokens), F32)
    for k in range(top):
        here = slot == info[k : k + 1, :]
        match += here.astype(F32)
        weight += jnp.where(here, info[top + k : top + k + 1, :], 0.0)
    match = jnp.where(same_step, match, 0.0)
    a = lax.broadcasted_iota(jnp.int32, (tokens, tokens), 0)
    b = lax.broadcasted_iota(jnp.int32, (tokens, tokens), 1)
    earlier = ((a % steps == b % steps) & (a < b)).astype(F32).astype(BF16)
    before = jnp.dot(match.astype(BF16), earlier, preferred_element_type=F32)
    taken = (match > 0.5) & (before.astype(jnp.int32) == place)
    weight_ref[...] = jnp.where(taken, weight, 0.0).astype(BF16)
    pick = taken.astype(F32)
    used = jnp.sum(pick, axis=1, keepdims=True)
    pick = pick.astype(BF16)
    got = got_ref[:, :piece]
    halves = 4
    size = count // halves
    copies = []
    lane = lax.broadcasted_iota(jnp.int32, (size, 128), 1)
    for i in range(halves):
        at = slice(i * size, (i + 1) * size)
        rows = jnp.dot(pick[at], got, preferred_element_type=F32)
        rows_ref[at, :128] = jnp.where((lane == 0) & (used[at] < 0.5), EMPTY, rows[:, :128]).astype(BF16)
        rows_ref[at, 128:] = rows[:, 128:].astype(BF16)
        out = pltpu.make_async_copy(rows_ref.at[at], rows_hbm.at[at], sems.at[i])
        out.start()
        copies.append(out)
    for out in copies:
        out.wait()


def split_body(steps, capacity, x_ref, *refs):
    first_ref, second_ref, count_ref = refs[-3:]
    total = x_ref.shape[0]
    half = total // 2
    head = x_ref[:, :128].astype(F32)
    used = (head[:, 0:1] < EMPTY).astype(F32)
    row = lax.broadcasted_iota(jnp.int32, (total, 128), 0)
    lane = lax.broadcasted_iota(jnp.int32, (total, 128), 1)
    counted = jnp.where((row // capacity) % steps == lane, used, 0.0)
    count_ref[...] = jnp.broadcast_to(jnp.sum(counted, axis=0, keepdims=True), count_ref.shape)
    head = jnp.where(lane == 0, head * used, head).astype(BF16)
    for i, out_ref in enumerate((first_ref, second_ref)):
        at = slice(i * half, (i + 1) * half)
        out_ref[:, :128] = head[at]
        out_ref[:, 128:] = x_ref[at, 128:]


def load_piece(here_ref, distance, weights, w_ref, sems):
    piece = w_ref.shape[1]
    dp = weights[0].shape[0] // piece
    block = lax.rem(here_ref[0] + distance, dp)
    at = pl.ds(pl.multiple_of(block * piece, piece), piece)
    loads = [pltpu.make_async_copy(w.at[at], w_ref.at[i], sems.at[i]) for i, w in enumerate(weights)]
    for load in loads:
        load.start()
    return loads


def beside(loads, w_ref):
    for load in loads:
        load.wait()
    gate_w = jnp.concatenate([w_ref[0], w_ref[2]], axis=1)
    up_w = jnp.concatenate([w_ref[1], w_ref[3]], axis=1)
    return gate_w, up_w


def products(first_ref, second_ref, gate_w, up_w):
    x = jnp.concatenate([first_ref[...], second_ref[...]], axis=0)
    gate = jnp.dot(x, gate_w, preferred_element_type=F32)
    up = jnp.dot(x, up_w, preferred_element_type=F32)
    return gate, up


def own_piece_body(here_ref, first_ref, second_ref, *refs):
    weights, (gate_out, up_out, w_ref, sems) = refs[:4], refs[4:]
    loads = load_piece(here_ref, 0, weights, w_ref, sems)
    gate_out[...], up_out[...] = products(first_ref, second_ref, *beside(loads, w_ref))


def near_pieces_body(
    here_ref, left_first, left_second, right_first, right_second, gate_in, up_in, *refs
):
    weights, (own_hbm, there_hbm) = refs[:4], refs[4:6]
    gate_out, up_out, far_out, down_out, w_ref, sems, down_sems = refs[6:]
    dp, hid, _ = own_hbm.shape
    down_loads = []
    for d in range(dp):
        for i, source in enumerate((own_hbm, there_hbm)):
            to = down_out.at[d, pl.ds(i * hid, hid)]
            down_loads.append(pltpu.make_async_copy(source.at[d], to, down_sems.at[d, i]))
    loads = [load_piece(here_ref, d, weights, w_ref.at[i], sems.at[i]) for i, d in enumerate((3, 1, 2))]
    for load in down_loads:
        load.start()
    gate, up = products(left_first, left_second, *beside(loads[0], w_ref.at[0]))
    gate_out[...] = gate_in[...] + gate
    up_out[...] = up_in[...] + up
    gate, up = products(right_first, right_second, *beside(loads[1], w_ref.at[1]))
    gate_out[...] += gate
    up_out[...] += up
    far_out[0], far_out[1] = beside(loads[2], w_ref.at[2])
    for load in down_loads:
        load.wait()


def last_piece_body(first_ref, second_ref, gate_in, up_in, far_ref, out_ref):
    gate, up = products(first_ref, second_ref, far_ref[0], far_ref[1])
    gate += gate_in[...]
    up += up_in[...]
    hidden = (gate / (1.0 + jnp.exp(-gate)) * up).astype(BF16)
    for i in range(out_ref.shape[0]):
        out_ref[i] = hidden


def down_body(here_ref, hid_ref, w_ref, out_hbm, out_ref, sems):
    dp, total, _ = hid_ref.shape
    pieces = 2
    size = total // pieces
    copies = []
    for i in range(pieces):
        at = slice(i * size, (i + 1) * size)
        out = jnp.zeros((size, out_ref.shape[1]), F32)
        for d in range(dp):
            block = lax.rem(here_ref[0] - d + dp, dp)
            out += jnp.dot(hid_ref[block, at], w_ref[d], preferred_element_type=F32)
        out_ref[at] = out.astype(BF16)
        copy = pltpu.make_async_copy(out_ref.at[at], out_hbm.at[at], sems.at[i])
        copy.start()
        copies.append(copy)
    for copy in copies:
        copy.wait()


def combine_body(weight_ref, got_ref, out_ref):
    dp, steps, _ = out_ref.shape
    out = lax.dot_general(
        weight_ref[...], got_ref[...], (((0,), (0,)), ((), ())), preferred_element_type=F32
    ).astype(BF16)
    for i in range(dp):
        out_ref[i] = out[i * steps : (i + 1) * steps]


def local(tokens, route_weight, expert_ids, replica, placement, w_gate, w_up, w_down):
    steps, _, width = tokens.shape
    top = expert_ids.shape[2]
    ep = lax.axis_size("ep")
    dp = lax.axis_size("dp")
    here = lax.axis_index("dp").astype(jnp.int32)
    slots = ep // 2
    piece = width // dp
    hid = w_gate.shape[2]
    capacity = 2
    per_slot = steps * capacity
    count = slots * per_slot
    same_core = [list(range(c, ep, 2)) for c in range(2)]
    swap = [(e, e ^ 1) for e in range(ep)]
    shape = jax.ShapeDtypeStruct
    here_at = here.reshape(1)

    (send,) = call(
        route_body,
        [shape((dp, steps, piece + 128), BF16)],
        [
            tokens.reshape(steps, width),
            route_weight.reshape(steps, top),
            expert_ids,
            replica,
            placement.T,
        ],
        in_specs=[HBM] * 5,
        scratch=[
            pltpu.VMEM((steps, width), BF16),
            pltpu.VMEM((steps, top), BF16),
            pltpu.VMEM((steps, 1, top), jnp.int32),
            pltpu.VMEM((steps, 1, top), jnp.int32),
            pltpu.VMEM(placement.shape[::-1], jnp.int32),
            pltpu.SemaphoreType.DMA((5,)),
        ],
    )
    got = lax.all_to_all(send, "dp", 0, 0)

    gate, up, down = w_gate[0], w_up[0], w_down[0]
    gate_there = lax.ppermute(gate, "ep", swap)
    up_there = lax.ppermute(up, "ep", swap)
    down_own = []
    for d in range(dp):
        block = lax.dynamic_slice(down, (0, lax.rem(here + d, dp) * piece), (hid, piece))
        down_own.append(lax.ppermute(block, "dp", [(x, (x + d) % dp) for x in range(dp)]) if d else block)
    down_own = jnp.stack(down_own)
    down_there = lax.ppermute(down_own, "ep", swap)

    rows, weight = call(
        functools.partial(pack_body, steps, capacity, top),
        [shape((count, piece), BF16), shape((count, dp * steps), BF16)],
        [got.reshape(dp * steps, piece + 128)],
        out_specs=[HBM, VMEM],
        scratch=[pltpu.VMEM((count, piece), BF16), pltpu.SemaphoreType.DMA((4,))],
    )
    arrived = lax.all_to_all(
        rows.reshape(slots, per_slot, piece), "ep", 0, 0, axis_index_groups=same_core
    ).reshape(count, piece)

    after = [down_there, gate_there, up_there]
    half = shape((count // 2, piece), BF16)
    first, second, used = call(
        functools.partial(split_body, steps, capacity),
        [half, half, shape((8, 128), F32)],
        [arrived, *after],
        in_specs=[VMEM, HBM, ANY, ANY],
    )
    ahead = [(x, (x + 1) % dp) for x in range(dp)]
    behind = [(x, (x - 1) % dp) for x in range(dp)]
    left_first = lax.ppermute(first, "dp", ahead)
    right_second = lax.ppermute(second, "dp", behind)
    left_second = lax.ppermute(second, "dp", ahead)
    right_first = lax.ppermute(first, "dp", behind)
    far_first = lax.ppermute(left_first, "dp", ahead)
    far_second = lax.ppermute(right_second, "dp", behind)
    weights = [gate, up, gate_there, up_there]
    sums = [shape((count, 2 * hid), F32)] * 2
    flops = 4 * count * piece * 2 * hid
    gate_sum, up_sum = call(
        own_piece_body,
        sums,
        [here_at, first, second, *weights],
        flops,
        in_specs=[SMEM, VMEM, VMEM] + [HBM] * 4,
        scratch=[pltpu.VMEM((4, piece, hid), BF16), pltpu.SemaphoreType.DMA((4,))],
    )
    gate_sum, up_sum, far_weights, down_weights = call(
        near_pieces_body,
        [*sums, shape((2, piece, 2 * hid), BF16), shape((dp, 2 * hid, piece), BF16)],
        [here_at, left_first, left_second, right_first, right_second, gate_sum, up_sum, *weights, down_own, down_there],
        2 * flops,
        in_specs=[SMEM] + [VMEM] * 6 + [HBM] * 6,
        scratch=[
            pltpu.VMEM((3, 4, piece, hid), BF16),
            pltpu.SemaphoreType.DMA((3, 4)),
            pltpu.SemaphoreType.DMA((dp, 2)),
        ],
        vmem=16,
    )
    (hidden,) = call(
        last_piece_body,
        [shape((dp, count, 2 * hid), BF16)],
        [far_first, far_second, gate_sum, up_sum, far_weights],
        flops,
    )
    hidden = lax.all_to_all(hidden, "dp", 0, 0)
    (out,) = call(
        down_body,
        [shape((count, piece), BF16)],
        [here_at, hidden, down_weights],
        4 * count * piece * dp * hid,
        in_specs=[SMEM, VMEM, VMEM],
        out_specs=[HBM],
        scratch=[pltpu.VMEM((count, piece), BF16), pltpu.SemaphoreType.DMA((2,))],
    )
    returned = lax.all_to_all(
        out.reshape(slots, per_slot, piece), "ep", 0, 0, axis_index_groups=same_core
    ).reshape(count, piece)
    (mine,) = call(
        combine_body, [shape((dp, steps, piece), BF16)], [weight, returned]
    )
    mine = lax.all_to_all(mine, "dp", 0, 0)
    moe_out = jnp.transpose(mine, (1, 0, 2)).reshape(steps, 1, width)

    used_there = lax.ppermute(used, "ep", swap)
    slot_rows = (used + used_there)[0, :steps].astype(jnp.int32).reshape(steps, 1)
    return (moe_out, slot_rows)


def solution(mesh):
    return jax.shard_map(
        local,
        mesh=mesh,
        in_specs=(
            P(None, ("ep", "dp"), None),
            P(None, ("ep", "dp"), None),
            P(None, ("ep", "dp"), None),
            P(None, ("ep", "dp"), None),
            P(),
            P("ep", None, "dp"),
            P("ep", None, "dp"),
            P("ep", "dp", None),
        ),
        out_specs=(P(None, ("ep", "dp"), None), P(None, "ep")),
        check_vma=False,
    )
```

```python
import functools

import jax
import jax.numpy as jnp
from jax import lax
from jax.experimental import pallas as pl
from jax.experimental.pallas import tpu as pltpu
from jax.sharding import PartitionSpec as P

BF16 = jnp.bfloat16
F32 = jnp.float32
EMPTY = 256.0


VMEM = pl.BlockSpec(memory_space=pltpu.VMEM)
HBM = pl.BlockSpec(memory_space=pltpu.HBM)
ANY = pl.BlockSpec(memory_space=pl.ANY)
SMEM = pl.BlockSpec(memory_space=pltpu.SMEM)


def call(body, outs, args, flops=0, in_specs=None, out_specs=None, scratch=(), vmem=12):
    if in_specs:
        args = [
            pltpu.with_memory_space_constraint(a, pltpu.HBM) if spec is HBM else a
            for a, spec in zip(args, in_specs, strict=True)
        ]
    moved = sum(a.size * a.dtype.itemsize for a in args)
    moved += sum(o.size * o.dtype.itemsize for o in outs)
    return pl.pallas_call(
        body,
        out_shape=tuple(
            pltpu.HBM(o.shape, o.dtype) if spec is HBM else o
            for o, spec in zip(outs, out_specs or [VMEM] * len(outs), strict=True)
        ),
        in_specs=in_specs or [VMEM] * len(args),
        out_specs=tuple(out_specs or [VMEM] * len(outs)),
        scratch_shapes=list(scratch),
        compiler_params=pltpu.CompilerParams(vmem_limit_bytes=vmem * 1024 * 1024),
        cost_estimate=pl.CostEstimate(flops=flops, bytes_accessed=moved, transcendentals=0),
    )(*args)


def route_body(
    tok_hbm, weight_hbm, ids_hbm, replica_hbm, place_hbm, send_ref,
    tok_ref, weight_ref, ids_ref, replica_ref, place_ref, sems,
):
    pairs = [
        (place_hbm, place_ref),
        (ids_hbm, ids_ref),
        (replica_hbm, replica_ref),
        (weight_hbm, weight_ref),
        (tok_hbm, tok_ref),
    ]
    copies = [pltpu.make_async_copy(a, b, sems.at[i]) for i, (a, b) in enumerate(pairs)]
    for c in copies:
        c.start()
    for c in copies:
        c.wait()
    dp, steps, wide = send_ref.shape
    piece = wide - 128
    top = ids_ref.shape[2]
    logical = place_ref.shape[1]
    ids, replica = ids_ref[:, 0, :], replica_ref[:, 0, :]
    first = jnp.broadcast_to(place_ref[0:1, :], (steps, logical))
    second = jnp.broadcast_to(place_ref[1:2, :], (steps, logical))
    expert = lax.broadcasted_iota(jnp.int32, (steps, logical), 1)
    lane = lax.broadcasted_iota(jnp.int32, (steps, 128), 1)
    tail = jnp.zeros((steps, 128), F32)
    for k in range(top):
        chosen = jnp.where(replica[:, k : k + 1] == 0, first, second)
        picked = jnp.where(expert == ids[:, k : k + 1], chosen, 0)
        slot = jnp.sum(picked.astype(F32), axis=1, keepdims=True)
        tail = jnp.where(lane == k, slot, tail)
        tail = jnp.where(lane == top + k, weight_ref[:, k : k + 1].astype(F32), tail)
    tail = tail.astype(BF16)
    for x in range(dp):
        send_ref[x, :, :piece] = tok_ref[:, x * piece : (x + 1) * piece]
        send_ref[x, :, piece:] = tail


def pack_body(steps, capacity, top, got_ref, rows_hbm, weight_ref, rows_ref, sems):
    tokens = got_ref.shape[0]
    piece = got_ref.shape[1] - 128
    count = rows_ref.shape[0]
    per_slot = steps * capacity
    info = got_ref[:, piece:].astype(F32).T
    row = lax.broadcasted_iota(jnp.int32, (count, tokens), 0)
    col = lax.broadcasted_iota(jnp.int32, (count, tokens), 1)
    slot = (row // per_slot).astype(F32)
    same_step = (row % per_slot) // capacity == col % steps
    place = row % capacity
    weight = jnp.zeros((count, tokens), F32)
    match = jnp.zeros((count, tokens), F32)
    for k in range(top):
        here = slot == info[k : k + 1, :]
        match += here.astype(F32)
        weight += jnp.where(here, info[top + k : top + k + 1, :], 0.0)
    match = jnp.where(same_step, match, 0.0)
    a = lax.broadcasted_iota(jnp.int32, (tokens, tokens), 0)
    b = lax.broadcasted_iota(jnp.int32, (tokens, tokens), 1)
    earlier = ((a % steps == b % steps) & (a < b)).astype(F32).astype(BF16)
    before = jnp.dot(match.astype(BF16), earlier, preferred_element_type=F32)
    taken = (match > 0.5) & (before.astype(jnp.int32) == place)
    weight_ref[...] = jnp.where(taken, weight, 0.0).astype(BF16)
    pick = taken.astype(F32)
    used = jnp.sum(pick, axis=1, keepdims=True)
    pick = pick.astype(BF16)
    got = got_ref[:, :piece]
    halves = 4
    size = count // halves
    copies = []
    lane = lax.broadcasted_iota(jnp.int32, (size, 128), 1)
    for i in range(halves):
        at = slice(i * size, (i + 1) * size)
        rows = jnp.dot(pick[at], got, preferred_element_type=F32)
        rows_ref[at, :128] = jnp.where((lane == 0) & (used[at] < 0.5), EMPTY, rows[:, :128]).astype(BF16)
        rows_ref[at, 128:] = rows[:, 128:].astype(BF16)
        out = pltpu.make_async_copy(rows_ref.at[at], rows_hbm.at[at], sems.at[i])
        out.start()
        copies.append(out)
    for out in copies:
        out.wait()


def split_body(steps, capacity, x_ref, *refs):
    first_ref, second_ref, count_ref = refs[-3:]
    total = x_ref.shape[0]
    half = total // 2
    head = x_ref[:, :128].astype(F32)
    used = (head[:, 0:1] < EMPTY).astype(F32)
    row = lax.broadcasted_iota(jnp.int32, (total, 128), 0)
    lane = lax.broadcasted_iota(jnp.int32, (total, 128), 1)
    counted = jnp.where((row // capacity) % steps == lane, used, 0.0)
    count_ref[...] = jnp.broadcast_to(jnp.sum(counted, axis=0, keepdims=True), count_ref.shape)
    head = jnp.where(lane == 0, head * used, head).astype(BF16)
    for i, out_ref in enumerate((first_ref, second_ref)):
        at = slice(i * half, (i + 1) * half)
        out_ref[:, :128] = head[at]
        out_ref[:, 128:] = x_ref[at, 128:]


def load_piece(here_ref, distance, weights, w_ref, sems):
    piece = w_ref.shape[1]
    dp = weights[0].shape[0] // piece
    block = lax.rem(here_ref[0] + distance, dp)
    at = pl.ds(pl.multiple_of(block * piece, piece), piece)
    loads = [pltpu.make_async_copy(w.at[at], w_ref.at[i], sems.at[i]) for i, w in enumerate(weights)]
    for load in loads:
        load.start()
    return loads


def beside(loads, w_ref):
    for load in loads:
        load.wait()
    gate_w = jnp.concatenate([w_ref[0], w_ref[2]], axis=1)
    up_w = jnp.concatenate([w_ref[1], w_ref[3]], axis=1)
    return gate_w, up_w


def products(first_ref, second_ref, gate_w, up_w):
    x = jnp.concatenate([first_ref[...], second_ref[...]], axis=0)
    gate = jnp.dot(x, gate_w, preferred_element_type=F32)
    up = jnp.dot(x, up_w, preferred_element_type=F32)
    return gate, up


def own_piece_body(here_ref, first_ref, second_ref, *refs):
    weights, (gate_out, up_out, w_ref, sems) = refs[:4], refs[4:]
    loads = load_piece(here_ref, 0, weights, w_ref, sems)
    gate_out[...], up_out[...] = products(first_ref, second_ref, *beside(loads, w_ref))


def near_pieces_body(
    here_ref, left_first, left_second, right_first, right_second, gate_in, up_in, *refs
):
    weights, (own_hbm, there_hbm) = refs[:4], refs[4:6]
    gate_out, up_out, far_out, down_out, w_ref, sems, down_sems = refs[6:]
    dp, hid, _ = own_hbm.shape
    down_loads = []
    for d in range(dp):
        for i, source in enumerate((own_hbm, there_hbm)):
            to = down_out.at[d, pl.ds(i * hid, hid)]
            down_loads.append(pltpu.make_async_copy(source.at[d], to, down_sems.at[d, i]))
    loads = [load_piece(here_ref, d, weights, w_ref.at[i], sems.at[i]) for i, d in enumerate((3, 1, 2))]
    for load in down_loads:
        load.start()
    gate, up = products(left_first, left_second, *beside(loads[0], w_ref.at[0]))
    gate_out[...] = gate_in[...] + gate
    up_out[...] = up_in[...] + up
    gate, up = products(right_first, right_second, *beside(loads[1], w_ref.at[1]))
    gate_out[...] += gate
    up_out[...] += up
    far_out[0], far_out[1] = beside(loads[2], w_ref.at[2])
    for load in down_loads:
        load.wait()


def finish(x_ref, gate_in, up_in, far_ref, at):
    gate = gate_in[at] + jnp.dot(x_ref[...], far_ref[0], preferred_element_type=F32)
    up = up_in[at] + jnp.dot(x_ref[...], far_ref[1], preferred_element_type=F32)
    return (gate / (1.0 + jnp.exp(-gate)) * up).astype(BF16)


def first_half_body(x_ref, gate_in, up_in, far_ref, out_ref):
    rows = x_ref.shape[0]
    out_ref[...] = finish(x_ref, gate_in, up_in, far_ref, slice(0, rows))


def second_half_body(x_ref, gate_in, up_in, far_ref, first_ref, out_ref):
    rows = x_ref.shape[0]
    hidden = finish(x_ref, gate_in, up_in, far_ref, slice(rows, 2 * rows))
    for i in range(out_ref.shape[0]):
        out_ref[i, :rows] = first_ref[...]
        out_ref[i, rows:] = hidden


def down_body(here_ref, hid_ref, w_ref, out_hbm, out_ref, sems):
    dp, total, _ = hid_ref.shape
    pieces = 2
    size = total // pieces
    copies = []
    for i in range(pieces):
        at = slice(i * size, (i + 1) * size)
        out = jnp.zeros((size, out_ref.shape[1]), F32)
        for d in range(dp):
            block = lax.rem(here_ref[0] - d + dp, dp)
            out += jnp.dot(hid_ref[block, at], w_ref[d], preferred_element_type=F32)
        out_ref[at] = out.astype(BF16)
        copy = pltpu.make_async_copy(out_ref.at[at], out_hbm.at[at], sems.at[i])
        copy.start()
        copies.append(copy)
    for copy in copies:
        copy.wait()


def combine_body(weight_ref, got_ref, out_ref):
    dp, steps, _ = out_ref.shape
    out = lax.dot_general(
        weight_ref[...], got_ref[...], (((0,), (0,)), ((), ())), preferred_element_type=F32
    ).astype(BF16)
    for i in range(dp):
        out_ref[i] = out[i * steps : (i + 1) * steps]


def local(tokens, route_weight, expert_ids, replica, placement, w_gate, w_up, w_down):
    steps, _, width = tokens.shape
    top = expert_ids.shape[2]
    ep = lax.axis_size("ep")
    dp = lax.axis_size("dp")
    here = lax.axis_index("dp").astype(jnp.int32)
    slots = ep // 2
    piece = width // dp
    hid = w_gate.shape[2]
    capacity = 2
    per_slot = steps * capacity
    count = slots * per_slot
    same_core = [list(range(c, ep, 2)) for c in range(2)]
    swap = [(e, e ^ 1) for e in range(ep)]
    shape = jax.ShapeDtypeStruct
    here_at = here.reshape(1)

    (send,) = call(
        route_body,
        [shape((dp, steps, piece + 128), BF16)],
        [
            tokens.reshape(steps, width),
            route_weight.reshape(steps, top),
            expert_ids,
            replica,
            placement.T,
        ],
        in_specs=[HBM] * 5,
        scratch=[
            pltpu.VMEM((steps, width), BF16),
            pltpu.VMEM((steps, top), BF16),
            pltpu.VMEM((steps, 1, top), jnp.int32),
            pltpu.VMEM((steps, 1, top), jnp.int32),
            pltpu.VMEM(placement.shape[::-1], jnp.int32),
            pltpu.SemaphoreType.DMA((5,)),
        ],
    )
    got = lax.all_to_all(send, "dp", 0, 0)

    gate, up, down = w_gate[0], w_up[0], w_down[0]
    gate_there = lax.ppermute(gate, "ep", swap)
    up_there = lax.ppermute(up, "ep", swap)
    down_own = []
    for d in range(dp):
        block = lax.dynamic_slice(down, (0, lax.rem(here + d, dp) * piece), (hid, piece))
        down_own.append(lax.ppermute(block, "dp", [(x, (x + d) % dp) for x in range(dp)]) if d else block)
    down_own = jnp.stack(down_own)
    down_there = lax.ppermute(down_own, "ep", swap)

    rows, weight = call(
        functools.partial(pack_body, steps, capacity, top),
        [shape((count, piece), BF16), shape((count, dp * steps), BF16)],
        [got.reshape(dp * steps, piece + 128)],
        out_specs=[HBM, VMEM],
        scratch=[pltpu.VMEM((count, piece), BF16), pltpu.SemaphoreType.DMA((4,))],
    )
    arrived = lax.all_to_all(
        rows.reshape(slots, per_slot, piece), "ep", 0, 0, axis_index_groups=same_core
    ).reshape(count, piece)

    after = [down_there, gate_there, up_there]
    half = shape((count // 2, piece), BF16)
    first, second, used = call(
        functools.partial(split_body, steps, capacity),
        [half, half, shape((8, 128), F32)],
        [arrived, *after],
        in_specs=[VMEM, HBM, ANY, ANY],
    )
    ahead = [(x, (x + 1) % dp) for x in range(dp)]
    behind = [(x, (x - 1) % dp) for x in range(dp)]
    left_first = lax.ppermute(first, "dp", ahead)
    right_second = lax.ppermute(second, "dp", behind)
    left_second = lax.ppermute(second, "dp", ahead)
    right_first = lax.ppermute(first, "dp", behind)
    far_first = lax.ppermute(left_first, "dp", ahead)
    far_second = lax.ppermute(right_second, "dp", behind)
    weights = [gate, up, gate_there, up_there]
    sums = [shape((count, 2 * hid), F32)] * 2
    flops = 4 * count * piece * 2 * hid
    gate_sum, up_sum = call(
        own_piece_body,
        sums,
        [here_at, first, second, *weights],
        flops,
        in_specs=[SMEM, VMEM, VMEM] + [HBM] * 4,
        scratch=[pltpu.VMEM((4, piece, hid), BF16), pltpu.SemaphoreType.DMA((4,))],
    )
    gate_sum, up_sum, far_weights, down_weights = call(
        near_pieces_body,
        [*sums, shape((2, piece, 2 * hid), BF16), shape((dp, 2 * hid, piece), BF16)],
        [here_at, left_first, left_second, right_first, right_second, gate_sum, up_sum, *weights, down_own, down_there],
        2 * flops,
        in_specs=[SMEM] + [VMEM] * 6 + [HBM] * 6,
        scratch=[
            pltpu.VMEM((3, 4, piece, hid), BF16),
            pltpu.SemaphoreType.DMA((3, 4)),
            pltpu.SemaphoreType.DMA((dp, 2)),
        ],
        vmem=16,
    )
    (first_hidden,) = call(
        first_half_body,
        [shape((count // 2, 2 * hid), BF16)],
        [far_first, gate_sum, up_sum, far_weights],
        flops // 2,
    )
    (hidden,) = call(
        second_half_body,
        [shape((dp, count, 2 * hid), BF16)],
        [far_second, gate_sum, up_sum, far_weights, first_hidden],
        flops // 2,
    )
    hidden = lax.all_to_all(hidden, "dp", 0, 0)
    (out,) = call(
        down_body,
        [shape((count, piece), BF16)],
        [here_at, hidden, down_weights],
        4 * count * piece * dp * hid,
        in_specs=[SMEM, VMEM, VMEM],
        out_specs=[HBM],
        scratch=[pltpu.VMEM((count, piece), BF16), pltpu.SemaphoreType.DMA((2,))],
    )
    returned = lax.all_to_all(
        out.reshape(slots, per_slot, piece), "ep", 0, 0, axis_index_groups=same_core
    ).reshape(count, piece)
    (mine,) = call(
        combine_body, [shape((dp, steps, piece), BF16)], [weight, returned]
    )
    mine = lax.all_to_all(mine, "dp", 0, 0)
    moe_out = jnp.transpose(mine, (1, 0, 2)).reshape(steps, 1, width)

    used_there = lax.ppermute(used, "ep", swap)
    slot_rows = (used + used_there)[0, :steps].astype(jnp.int32).reshape(steps, 1)
    return (moe_out, slot_rows)


def solution(mesh):
    return jax.shard_map(
        local,
        mesh=mesh,
        in_specs=(
            P(None, ("ep", "dp"), None),
            P(None, ("ep", "dp"), None),
            P(None, ("ep", "dp"), None),
            P(None, ("ep", "dp"), None),
            P(),
            P("ep", None, "dp"),
            P("ep", None, "dp"),
            P("ep", "dp", None),
        ),
        out_specs=(P(None, ("ep", "dp"), None), P(None, "ep")),
        check_vma=False,
    )
```
